32 devices in a mesh: node: 4 (over z), bond: 8 (over y, x, core).
Axes of the slice: x: 2, y: 2, z: 4, core: 2. Of those that a mesh axis runs over, the one named last changes fastest.
Arguments:
- bottom_nodes: float32 [4, 128, 128, 128], P('node', 'bond'), may hold values from -0.046875 to 0.046875
- upper_nodes: float32 [4, 128, 128, 128], P(None, 'bond', 'node'), may hold values from -0.046875 to 0.046875
- leaf_up: float32 [4, 3, 2, 128, 128], P('node'), may hold values from -2 to 3
- outside_env: float32 [3, 128, 128], replicated, may hold values from -2 to 3
- top_env: float32 [3, 128, 128], replicated, may hold values from -2 to 3
Outputs:
- leaf_down: float32 [4, 3, 2, 128, 128], P('node', None, None, 'bond')
- subtree_env: float32 [3, 128, 128], replicated
The draws below stay inside these ranges and needn't reach their ends.
All inputs are finite; a program needn't handle non-finite values.
Results may differ from the reference program's by a relative error of at most 0.0001.
Values sent between devices are 32-bit elements; how exact they have to be, the bound alone decides.
A program may use at most 128 MiB of HBM per device.

```python
import math
import jax
import jax.numpy as jnp
from jax import lax

D = 128
OPS = 3
NODES = 4


def env_matrix(key, shape):
    identity = jnp.eye(D, dtype=jnp.float32)
    spread = jnp.clip(jax.random.normal(key, shape, jnp.float32), -6.0, 6.0) * (3.0 / math.sqrt(D))
    return identity + spread


def draw_leaf_up(key, part):
    return env_matrix(jax.random.fold_in(key, 11), (NODES, OPS, 2, D, D))


def draw_outside_env(key, part):
    return env_matrix(jax.random.fold_in(key, 23), (OPS, D, D))


def draw_top_env(key, part):
    return env_matrix(jax.random.fold_in(key, 37), (OPS, D, D))


def steps_of(stream_key, shape, pieces, low, high):
    def one(axis_at, blocks):
        heights = jax.random.uniform(jax.random.fold_in(jax.random.fold_in(stream_key, 6), axis_at), (blocks,), jnp.float32, low / len(pieces), high / len(pieces))
        return jnp.repeat(jnp.exp(heights), shape[axis_at] // blocks).reshape((-1,) + (1,) * (len(shape) - axis_at - 1))

    loudness = one(*pieces[0])
    for cut in pieces[1:]:
        loudness = loudness * one(*cut)
    return loudness


def normal_values(stream_key, extent, deviation, limit, cuts=(), kind=jnp.bfloat16):
    gain = steps_of(stream_key, extent, cuts, -0.22, 0.18) if cuts else 1.0
    entries = jax.random.normal(stream_key, extent, jnp.float32) * deviation * gain
    return jnp.minimum(jnp.maximum(entries, -limit), limit).astype(kind)


def setup_inputs(seed: int = 0) -> dict:
    splits = jax.random.split(jax.random.key(seed), 6)
    return {
        "bottom_nodes": normal_values(splits[0], (NODES, D, D, D), (D * D) ** -0.5, 0.046875, ((0, 4), (1, 8)), jnp.float32),
        "upper_nodes": normal_values(splits[1], (NODES, D, D, D), (D * D) ** -0.5, 0.046875, ((1, 8), (2, 4)), jnp.float32),
        "leaf_up": draw_leaf_up(jax.random.fold_in(splits[5], 71), 0),
        "outside_env": draw_outside_env(jax.random.fold_in(splits[5], 71), 0),
        "top_env": draw_top_env(jax.random.fold_in(splits[5], 71), 0),
    }


highest = lax.Precision.HIGHEST


def grow_env(tensor, left_env, right_env):
    middle = jnp.einsum('kac,pcd->kpad', left_env, tensor, precision=highest)
    product = jnp.einsum('kpad,kbd->kpab', middle, right_env, precision=highest)
    return jnp.einsum('pab,kqab->kpq', tensor, product, precision=highest)


def split_env(tensor, above, left_env, right_env):
    worked = jnp.einsum('kpq,qcd->kpcd', above, tensor, precision=highest)
    first = jnp.einsum('kpcd,kbd->kpcb', worked, right_env, precision=highest)
    first_env = jnp.einsum('pab,kpcb->kac', tensor, first, precision=highest)
    second = jnp.einsum('kac,kpcd->kpad', left_env, worked, precision=highest)
    second_env = jnp.einsum('pab,kpad->kbd', tensor, second, precision=highest)
    return first_env, second_env


def reference(bottom_nodes, upper_nodes, leaf_up, outside_env, top_env):
    nodes = NODES
    ups = [None] * (2 * nodes)
    for index in range(nodes):
        ups[nodes + index] = grow_env(bottom_nodes[index], leaf_up[index, :, 0], leaf_up[index, :, 1])
    for slot in range(nodes - 1, 0, -1):
        ups[slot] = grow_env(upper_nodes[slot], ups[2 * slot], ups[2 * slot + 1])
    downs = [None] * (2 * nodes)
    downs[1] = split_env(upper_nodes[0], top_env, ups[1], outside_env)[0]
    for slot in range(1, nodes):
        first_env, second_env = split_env(upper_nodes[slot], downs[slot], ups[2 * slot], ups[2 * slot + 1])
        downs[2 * slot] = first_env
        downs[2 * slot + 1] = second_env
    leaves = []
    for index in range(nodes):
        first_env, second_env = split_env(bottom_nodes[index], downs[nodes + index], leaf_up[index, :, 0], leaf_up[index, :, 1])
        leaves.append(jnp.stack([first_env, second_env], 1))
    return jnp.stack(leaves), ups[1]
```

```python
import functools

import jax
import jax.numpy as jnp
from jax import lax
from jax.experimental import pallas as pl
from jax.experimental.pallas import tpu as pltpu
from jax.sharding import PartitionSpec as P

MESH = pl.DeviceIdType.MESH
NN = (((1,), (0,)), ((), ()))
NT = (((1,), (1,)), ((), ()))
f32 = jnp.float32


def split(x):
    high = x.astype(jnp.bfloat16)
    return high, (x - high.astype(f32)).astype(jnp.bfloat16)


def mm(a, b, dims):
    def dot(u, v):
        return lax.dot_general(u, v, dims, preferred_element_type=f32)

    return dot(a[0], b[0]) + (dot(a[0], b[1]) + dot(a[1], b[0]))


def loop(start, stop, body):
    def step(i, carry):
        body(i)
        return carry

    lax.fori_loop(start, stop, step, 0)


def kernel(
    nodes, bonds,
    bottom, upper, leaf, outside, top,
    leaf_out, root_out,
    all_low, all_up, own_up, grown, worked, side_r, side_l, childs, gram_s, part, got, above, above_s, root,
    far_s, near_s, piece_r, swap_s, swap_r, child_s, child_r, sum_s, sum_r, env_s, env_r, root_s, root_r,
):
    z, j = lax.axis_index("node"), lax.axis_index("bond")
    me = z * bonds + j
    total = nodes * bonds
    chips = bonds // 2
    twin = j + 1 - 2 * lax.rem(j, 2)
    rows, width = bottom.shape[1], bottom.shape[2]
    ops = leaf.shape[1]
    cols = upper.shape[2]
    block = rows * width
    packed = ops * rows
    mine = pl.ds(pl.multiple_of(j * rows, rows), rows)

    def remote(src, dst, send, recv, plane, bond):
        return pltpu.make_async_remote_copy(
            src_ref=src, dst_ref=dst, send_sem=send, recv_sem=recv,
            device_id=(plane, bond), device_id_type=MESH,
        )

    barrier = pltpu.get_barrier_semaphore()

    def greet(m):
        t = lax.rem(me + m, total)
        pl.semaphore_signal(barrier, inc=1, device_id=(t // bonds, lax.rem(t, bonds)), device_id_type=MESH)

    loop(1, total, greet)

    def turn(src, dst):
        def one(p):
            dst[pl.ds(j * block + p, width, stride=rows), :] = src[p]

        loop(0, rows, one)

    turn(bottom.at[0], all_low)
    pl.semaphore_wait(barrier, total - 1)

    def piece(whole, i):
        return whole.at[pl.ds(pl.multiple_of(i * block, block), block), :]

    def far_copy(g, whole, m):
        return remote(piece(whole, j), piece(whole, j), far_s.at[g, m], piece_r.at[g, j], z, lax.rem(j + 2 * m, bonds))

    def near_copy(g, whole, m):
        i = lax.rem(j + 2 * m, bonds)
        return remote(piece(whole, i), piece(whole, i), near_s.at[g, m], piece_r.at[g, i], z, twin)

    def arrived(g, whole, i):
        remote(piece(whole, i), piece(whole, i), far_s.at[g, 0], piece_r.at[g, i], z, twin).wait_recv()

    def gather_start(g, whole):
        loop(1, chips, lambda m: far_copy(g, whole, m).start())
        near_copy(g, whole, 0).start()

    def gather_pass(g, whole):
        def one(m):
            arrived(g, whole, lax.rem(j + 2 * m, bonds))
            near_copy(g, whole, m).start()

        loop(1, chips, one)

    def gather_end(g, whole):
        loop(0, chips, lambda m: arrived(g, whole, lax.rem(twin + 2 * m, bonds)))

    def gather_sent(g, whole):
        loop(1, chips, lambda m: far_copy(g, whole, m).wait_send())
        loop(0, chips, lambda m: near_copy(g, whole, m).wait_send())

    gather_start(0, all_low)

    def swap(m):
        t = lax.rem(z + m, nodes)
        return remote(
            upper.at[t], own_up.at[:, pl.ds(pl.multiple_of(z * cols, cols), cols), :],
            swap_s.at[m], swap_r.at[z], t, j,
        )

    loop(1, nodes, lambda m: swap(m).start())

    def keep(p):
        own_up[p, pl.ds(pl.multiple_of(z * cols, cols), cols), :] = upper[z, p]

    loop(0, rows, keep)

    def prepare(g, x_of, left_of, right_of):
        def operator(k):
            left = left_of(k)
            l, lt, r = split(left), split(left.T), split(right_of(k))

            def one(p, carry):
                x = x_of(p)
                u = mm(split(x), r, NN)
                side_r[g, k, p] = u
                side_l[g, k, p] = mm(split(x.T), l, NN)
                grown[pl.ds(k * rows + p, width, stride=packed), :] = mm(lt, split(u), NN)
                return carry

            lax.fori_loop(0, rows, one, 0, unroll=2)

        loop(0, ops, operator)

    def column(whole, c):
        parts = [whole[pl.ds(pl.multiple_of(i * block + c * rows, rows), rows), :] for i in range(bonds)]
        return jnp.concatenate(parts, axis=0)

    def at_column(c):
        return pl.ds(pl.multiple_of(c * packed, packed), packed)

    def gram(g, whole):
        def one(c, acc):
            return acc + mm(split(grown[at_column(c), :]), split(column(whole, c)), NT)

        out = lax.fori_loop(0, width, one, jnp.zeros((packed, width), f32), unroll=8)
        gram_s[g] = out.reshape(ops, rows, width)

    def down(g, whole, env):
        e = split(env.reshape(packed, width))

        def one(c, carry):
            worked[at_column(c), :] = mm(e, split(column(whole, c)), NN)
            return carry

        lax.fori_loop(0, width, one, 0, unroll=8)

        def operator(k):
            def inner(p, carry):
                first, second = carry
                w = split(worked[pl.ds(k * rows + p, width, stride=packed), :])
                first = first + mm(split(side_r[g, k, p]), w, NT)
                second = second + mm(split(side_l[g, k, p]), w, NN)
                return first, second

            zero = jnp.zeros((width, width), f32)
            first, second = lax.fori_loop(0, rows, inner, (zero, zero), unroll=2)
            part[g, 0, k] = first
            part[g, 1, k] = second

        loop(0, ops, operator)

    def sum_copy(g, m):
        i = lax.rem(j + m, bonds)
        return remote(
            part.at[g, :, :, pl.ds(pl.multiple_of(i * rows, rows), rows), :], got.at[g, j],
            sum_s.at[g, m], sum_r.at[g, j], z, i,
        )

    def plane_sum(g):
        loop(1, bonds, lambda m: sum_copy(g, m).start())

        def add(m, acc):
            i = lax.rem(j + m, bonds)
            remote(
                part.at[g, :, :, mine, :], got.at[g, i], sum_s.at[g, 0], sum_r.at[g, i], z, twin
            ).wait_recv()
            return acc + got[g, i]

        return lax.fori_loop(1, bonds, add, part[g, :, :, mine, :])

    def child_copy(g, number, i):
        return remote(
            gram_s.at[g], childs.at[lax.rem(number, 2), :, mine, :],
            child_s.at[g, i], child_r.at[lax.rem(number, 2), j], number // 2, i,
        )

    def child_send(g, number):
        def one(i):
            own = (number // 2) * bonds + i == me

            @pl.when(own)
            def _():
                childs[lax.rem(number, 2), :, mine, :] = gram_s[g]

            @pl.when(jnp.logical_not(own))
            def _():
                child_copy(g, number, i).start()

        loop(0, bonds, one)

    def child_sent(g, number):
        def one(i):
            @pl.when((number // 2) * bonds + i != me)
            def _():
                child_copy(g, number, i).wait_send()

        loop(0, bonds, one)

    def child_wait():
        for first in range(2):
            number = 2 * z + first
            plane = jnp.where(number >= nodes, number - nodes, number)

            def one(i):
                @pl.when(plane * bonds + i != me)
                def _():
                    remote(
                        gram_s.at[0], childs.at[first, :, pl.ds(pl.multiple_of(i * rows, rows), rows), :],
                        child_s.at[0, 0], child_r.at[first, i], z, twin,
                    ).wait_recv()

            loop(0, bonds, one)

    def env_target(first):
        number = jnp.where(z == 0, 1, 2 * z + first)
        low = (number >= nodes).astype(jnp.int32)
        return number - low * nodes, low

    def env_copy(first):
        plane, low = env_target(first)
        return remote(above_s.at[first], above.at[low], env_s.at[first], env_r.at[low], plane, j)

    def env_wait(low):
        remote(above_s.at[0], above.at[low], env_s.at[0], env_r.at[low], z, twin).wait_recv()

    prepare(0, lambda p: bottom[0, p], lambda k: leaf[0, k, 0], lambda k: leaf[0, k, 1])

    gather_pass(0, all_low)

    def swapped(m):
        i = lax.rem(z + m, nodes)
        remote(
            upper.at[0], own_up.at[:, pl.ds(pl.multiple_of(i * cols, cols), cols), :],
            swap_s.at[0], swap_r.at[i], lax.rem(z + 1, nodes), j,
        ).wait_recv()

    loop(1, nodes, swapped)
    turn(own_up, all_up)
    gather_start(1, all_up)
    gather_end(0, all_low)
    gram(0, all_low)
    child_send(0, nodes + z)

    gather_pass(1, all_up)
    gather_end(1, all_up)

    @pl.when(z == 0)
    def _():
        childs[0] = outside[...]
        childs[1] = outside[...]
        above[0] = top[:, mine, :]

    @pl.when(z > 0)
    def _():
        child_wait()

    prepare(1, lambda p: own_up[p], lambda k: childs[0, k], lambda k: childs[1, k])

    @pl.when(z > 1)
    def _():
        gram(1, all_up)
        child_send(1, z)

    @pl.when(z > 0)
    def _():
        env_wait(0)

    down(1, all_up, above[0])
    above_s[...] = plane_sum(1)
    for first in range(2):
        plane, low = env_target(first)
        live = jnp.logical_or(z > 0, first == 0)

        @pl.when(jnp.logical_and(live, plane == z))
        def _():
            above[1] = above_s[first]

        @pl.when(jnp.logical_and(live, plane != z))
        def _():
            env_copy(first).start()

    def root_copy(m):
        t = lax.rem(me + m, total)
        return remote(
            gram_s.at[1], root.at[:, mine, :], root_s.at[m], root_r.at[j], t // bonds, lax.rem(t, bonds)
        )

    @pl.when(z == 1)
    def _():
        gram(1, all_up)
        root[:, mine, :] = gram_s[1]
        loop(1, total, lambda m: root_copy(m).start())

    @pl.when((nodes + z) // 2 != z)
    def _():
        env_wait(1)

    down(0, all_low, above[1])
    ours = plane_sum(0)
    for first in range(2):
        for k in range(ops):
            leaf_out[0, k, first] = ours[first, k]

    def root_wait(i):
        @pl.when(bonds + i != me)
        def _():
            remote(
                gram_s.at[1], root.at[:, pl.ds(pl.multiple_of(i * rows, rows), rows), :],
                root_s.at[0], root_r.at[i], z, twin,
            ).wait_recv()

    loop(0, bonds, root_wait)
    root_out[...] = root[...]

    gather_sent(0, all_low)
    gather_sent(1, all_up)
    loop(1, nodes, lambda m: swap(m).wait_send())
    child_sent(0, nodes + z)

    @pl.when(z > 1)
    def _():
        child_sent(1, z)

    for g in range(2):
        loop(1, bonds, lambda m: sum_copy(g, m).wait_send())
    for first in range(2):
        plane, low = env_target(first)

        @pl.when(jnp.logical_and(jnp.logical_or(z > 0, first == 0), plane != z))
        def _():
            env_copy(first).wait_send()

    @pl.when(z == 1)
    def _():
        loop(1, total, lambda m: root_copy(m).wait_send())


def solution(mesh):
    nodes, bonds = mesh.shape["node"], mesh.shape["bond"]

    def local(bottom, upper, leaf, outside, top):
        rows, width = bottom.shape[1], bottom.shape[2]
        ops = leaf.shape[1]
        dma = pltpu.SemaphoreType.DMA
        return pl.pallas_call(
            functools.partial(kernel, nodes, bonds),
            out_shape=(
                jax.ShapeDtypeStruct((1, ops, 2, rows, width), f32),
                jax.ShapeDtypeStruct((ops, width, width), f32),
            ),
            in_specs=[pl.BlockSpec(memory_space=pltpu.VMEM)] * 5,
            out_specs=(pl.BlockSpec(memory_space=pltpu.VMEM),) * 2,
            scratch_shapes=[
                pltpu.VMEM((bonds * rows * width, width), f32),
                pltpu.VMEM((bonds * rows * width, width), f32),
                pltpu.VMEM((rows, width, width), f32),
                pltpu.VMEM((width * ops * rows, width), f32),
                pltpu.VMEM((width * ops * rows, width), f32),
                pltpu.VMEM((2, ops, rows, width, width), f32),
                pltpu.VMEM((2, ops, rows, width, width), f32),
                pltpu.VMEM((2, ops, width, width), f32),
                pltpu.VMEM((2, ops, rows, width), f32),
                pltpu.VMEM((2, 2, ops, width, width), f32),
                pltpu.VMEM((2, bonds, 2, ops, rows, width), f32),
                pltpu.VMEM((2, ops, rows, width), f32),
                pltpu.VMEM((2, ops, rows, width), f32),
                pltpu.VMEM((ops, width, width), f32),
                dma((2, bonds // 2)),
                dma((2, bonds // 2)),
                dma((2, bonds)),
                dma((nodes,)),
                dma((nodes,)),
                dma((2, bonds)),
                dma((2, bonds)),
                dma((2, bonds)),
                dma((2, bonds)),
                dma((2,)),
                dma((2,)),
                dma((nodes * bonds,)),
                dma((bonds,)),
            ],
            compiler_params=pltpu.CompilerParams(
                collective_id=0, has_side_effects=True, vmem_limit_bytes=56 * 1024 * 1024
            ),
        )(bottom, upper, leaf, outside, top)

    placed = (
        P("node", "bond", None, None),
        P(None, "bond", "node", None),
        P("node", None, None, None, None),
        P(),
        P(),
    )
    return jax.shard_map(
        local,
        mesh=mesh,
        in_specs=placed,
        out_specs=(P("node", None, None, "bond", None), P()),
        check_vma=False,
    )
```

```python
import functools

import jax
import jax.numpy as jnp
from jax import lax
from jax.experimental import pallas as pl
from jax.experimental.pallas import tpu as pltpu
from jax.sharding import PartitionSpec as P

MESH = pl.DeviceIdType.MESH
NN = (((1,), (0,)), ((), ()))
NT = (((1,), (1,)), ((), ()))
f32 = jnp.float32


def split(x):
    high = x.astype(jnp.bfloat16)
    return high, (x - high.astype(f32)).astype(jnp.bfloat16)


def dot(a, b, dims=NN):
    return lax.dot_general(a, b, dims, preferred_element_type=f32)


def wide(x):
    return jnp.concatenate(split(x), axis=1)


def twice(x):
    w = wide(x)
    return jnp.concatenate([w, w], axis=0)


def halves(out):
    half = out.shape[1] // 2
    return out[:, :half] + out[:, half:]


def quarters(out):
    half = out.shape[0] // 2
    return halves(out[:half] + out[half:])


def loop(start, stop, body):
    def step(i, carry):
        body(i)
        return carry

    lax.fori_loop(start, stop, step, 0)


def kernel(
    nodes, bonds,
    bottom, upper, leaf, outside, top,
    leaf_out, root_out,
    all_low, all_up, own_up, grown, worked, side_r, side_l, long_l, long_r, childs, gram_s, part, got, above, above_s, root,
    far_s, near_s, piece_r, swap_s, swap_r, child_s, child_r, sum_s, sum_r, env_s, env_r, root_s, root_r,
):
    z, j = lax.axis_index("node"), lax.axis_index("bond")
    me = z * bonds + j
    total = nodes * bonds
    chips = bonds // 2
    twin = j + 1 - 2 * lax.rem(j, 2)
    rows, width = bottom.shape[1], bottom.shape[2]
    ops = leaf.shape[1]
    cols = upper.shape[2]
    block = rows * width
    packed = ops * rows
    mine = pl.ds(pl.multiple_of(j * rows, rows), rows)

    def remote(src, dst, send, recv, plane, bond):
        return pltpu.make_async_remote_copy(
            src_ref=src, dst_ref=dst, send_sem=send, recv_sem=recv,
            device_id=(plane, bond), device_id_type=MESH,
        )

    barrier = pltpu.get_barrier_semaphore()

    def greet(m):
        t = lax.rem(me + m, total)
        pl.semaphore_signal(barrier, inc=1, device_id=(t // bonds, lax.rem(t, bonds)), device_id_type=MESH)

    loop(1, total, greet)

    def turn(src, dst):
        def one(p):
            dst[pl.ds(j * block + p, width, stride=rows), :] = src[p]

        loop(0, rows, one)

    turn(bottom.at[0], all_low)
    pl.semaphore_wait(barrier, total - 1)

    def piece(whole, i):
        return whole.at[pl.ds(pl.multiple_of(i * block, block), block), :]

    def far_copy(g, whole, m):
        return remote(piece(whole, j), piece(whole, j), far_s.at[g, m], piece_r.at[g, j], z, lax.rem(j + 2 * m, bonds))

    def near_copy(g, whole, m):
        i = lax.rem(j + 2 * m, bonds)
        return remote(piece(whole, i), piece(whole, i), near_s.at[g, m], piece_r.at[g, i], z, twin)

    def arrived(g, whole, i):
        remote(piece(whole, i), piece(whole, i), far_s.at[g, 0], piece_r.at[g, i], z, twin).wait_recv()

    def gather_start(g, whole):
        loop(1, chips, lambda m: far_copy(g, whole, m).start())
        near_copy(g, whole, 0).start()

    def gather_pass(g, whole):
        def one(m):
            arrived(g, whole, lax.rem(j + 2 * m, bonds))
            near_copy(g, whole, m).start()

        loop(1, chips, one)

    def gather_end(g, whole):
        loop(0, chips, lambda m: arrived(g, whole, lax.rem(twin + 2 * m, bonds)))

    def gather_sent(g, whole):
        loop(1, chips, lambda m: far_copy(g, whole, m).wait_send())
        loop(0, chips, lambda m: near_copy(g, whole, m).wait_send())

    gather_start(0, all_low)

    def swap(m):
        t = lax.rem(z + m, nodes)
        return remote(
            upper.at[t], own_up.at[:, pl.ds(pl.multiple_of(z * cols, cols), cols), :],
            swap_s.at[m], swap_r.at[z], t, j,
        )

    loop(1, nodes, lambda m: swap(m).start())

    def keep(p):
        own_up[p, pl.ds(pl.multiple_of(z * cols, cols), cols), :] = upper[z, p]

    loop(0, rows, keep)

    def grow(x_of, left_of, right_of):
        lefts = wide(jnp.concatenate([left_of(k).T for k in range(ops)], axis=0))

        def one(p, carry):
            out = halves(dot(lefts, twice(x_of(p))))
            for k in range(ops):
                grown[pl.ds(k * block + p, width, stride=rows), :] = out[k * width : (k + 1) * width]
            return carry

        lax.fori_loop(0, rows, one, 0, unroll=2)
        step = 4 * width
        for k in range(ops):
            right = twice(right_of(k))

            def chunk(i, carry):
                at = pl.ds(pl.multiple_of(k * block + i * step, step), step)
                grown[at, :] = halves(dot(wide(grown[at, :]), right))
                return carry

            lax.fori_loop(0, block // step, chunk, 0)

    def sides(g, x_of, left_of, right_of):
        rights = wide(jnp.concatenate([right_of(k).T for k in range(ops)], axis=0))

        def one(p, carry):
            turned = x_of(p).T
            out = halves(dot(rights, twice(turned)))
            turned_wide = wide(turned)
            at = pl.ds(pl.multiple_of(p * width, width), width)
            for k in range(ops):
                side_r[g, k, at, :] = wide(out[k * width : (k + 1) * width])
                high, low = split(halves(dot(turned_wide, twice(left_of(k)))))
                side_l[g, k, :width, at] = high
                side_l[g, k, width:, at] = low
            return carry

        lax.fori_loop(0, rows, one, 0, unroll=2)

    def column(whole, c):
        parts = [whole[pl.ds(pl.multiple_of(i * block + c * rows, rows), rows), :] for i in range(bonds)]
        return jnp.concatenate(parts, axis=0)

    def gram(g, whole):
        def slab(c):
            parts = [
                grown[pl.ds(pl.multiple_of(k * block + c * rows, rows), rows), :] for k in range(ops)
            ]
            return jnp.concatenate(split(jnp.concatenate(parts, axis=0)), axis=0)

        def one(i, acc):
            t = jnp.concatenate([slab(2 * i), slab(2 * i + 1)], axis=1)
            x = jnp.concatenate(
                [jnp.concatenate(split(column(whole, 2 * i + d)), axis=0) for d in range(2)], axis=1
            )
            return acc + dot(t, x, NT)

        zero = jnp.zeros((2 * packed, 2 * width), f32)
        out = lax.fori_loop(0, width // 2, one, zero, unroll=4)
        gram_s[g] = quarters(out).reshape(ops, rows, width)

    def down(g, whole, env):
        e = jnp.concatenate(split(env.reshape(packed, width)), axis=0)

        def one(c, carry):
            at = pl.ds(pl.multiple_of(c * packed, packed), packed)
            worked[at, :] = quarters(dot(e, wide(column(whole, c))))
            return carry

        lax.fori_loop(0, width, one, 0, unroll=8)

        def operator(k):
            def fill(p, carry):
                high, low = split(worked[pl.ds(k * rows + p, width, stride=packed), :])
                at = pl.ds(pl.multiple_of(p * width, width), width)
                long_l[:width, at] = high
                long_l[width:, at] = low
                long_r[at, :width] = high
                long_r[at, width:] = low
                return carry

            lax.fori_loop(0, rows, fill, 0, unroll=4)
            part[g, 0, k] = quarters(dot(long_l[...], side_r[g, k])).T
            part[g, 1, k] = quarters(dot(side_l[g, k], long_r[...]))

        loop(0, ops, operator)

    def sum_copy(g, m):
        i = lax.rem(j + m, bonds)
        return remote(
            part.at[g, :, :, pl.ds(pl.multiple_of(i * rows, rows), rows), :], got.at[g, j],
            sum_s.at[g, m], sum_r.at[g, j], z, i,
        )

    def plane_sum(g):
        loop(1, bonds, lambda m: sum_copy(g, m).start())

        def add(m, acc):
            i = lax.rem(j + m, bonds)
            remote(
                part.at[g, :, :, mine, :], got.at[g, i], sum_s.at[g, 0], sum_r.at[g, i], z, twin
            ).wait_recv()
            return acc + got[g, i]

        return lax.fori_loop(1, bonds, add, part[g, :, :, mine, :])

    def child_copy(g, number, i):
        return remote(
            gram_s.at[g], childs.at[lax.rem(number, 2), :, mine, :],
            child_s.at[g, i], child_r.at[lax.rem(number, 2), j], number // 2, i,
        )

    def child_send(g, number):
        def one(i):
            own = (number // 2) * bonds + i == me

            @pl.when(own)
            def _():
                childs[lax.rem(number, 2), :, mine, :] = gram_s[g]

            @pl.when(jnp.logical_not(own))
            def _():
                child_copy(g, number, i).start()

        loop(0, bonds, one)

    def child_sent(g, number):
        def one(i):
            @pl.when((number // 2) * bonds + i != me)
            def _():
                child_copy(g, number, i).wait_send()

        loop(0, bonds, one)

    def child_wait():
        for first in range(2):
            number = 2 * z + first
            plane = jnp.where(number >= nodes, number - nodes, number)

            def one(i):
                @pl.when(plane * bonds + i != me)
                def _():
                    remote(
                        gram_s.at[0], childs.at[first, :, pl.ds(pl.multiple_of(i * rows, rows), rows), :],
                        child_s.at[0, 0], child_r.at[first, i], z, twin,
                    ).wait_recv()

            loop(0, bonds, one)

    def env_target(first):
        number = jnp.where(z == 0, 1, 2 * z + first)
        low = (number >= nodes).astype(jnp.int32)
        return number - low * nodes, low

    def env_copy(first):
        plane, low = env_target(first)
        return remote(above_s.at[first], above.at[low], env_s.at[first], env_r.at[low], plane, j)

    def env_wait(low):
        remote(above_s.at[0], above.at[low], env_s.at[0], env_r.at[low], z, twin).wait_recv()

    grow(lambda p: bottom[0, p], lambda k: leaf[0, k, 0], lambda k: leaf[0, k, 1])
    sides(0, lambda p: bottom[0, p], lambda k: leaf[0, k, 0], lambda k: leaf[0, k, 1])

    gather_pass(0, all_low)

    def swapped(m):
        i = lax.rem(z + m, nodes)
        remote(
            upper.at[0], own_up.at[:, pl.ds(pl.multiple_of(i * cols, cols), cols), :],
            swap_s.at[0], swap_r.at[i], lax.rem(z + 1, nodes), j,
        ).wait_recv()

    loop(1, nodes, swapped)
    turn(own_up, all_up)
    gather_start(1, all_up)
    gather_end(0, all_low)
    gram(0, all_low)
    child_send(0, nodes + z)

    gather_pass(1, all_up)
    gather_end(1, all_up)

    @pl.when(z == 0)
    def _():
        childs[0] = outside[...]
        childs[1] = outside[...]
        above[0] = top[:, mine, :]

    @pl.when(z > 0)
    def _():
        child_wait()

    def grow_up():
        grow(lambda p: own_up[p], lambda k: childs[0, k], lambda k: childs[1, k])

    @pl.when(z > 1)
    def _():
        grow_up()
        gram(1, all_up)
        child_send(1, z)

    sides(1, lambda p: own_up[p], lambda k: childs[0, k], lambda k: childs[1, k])

    @pl.when(z > 0)
    def _():
        env_wait(0)

    down(1, all_up, above[0])
    above_s[...] = plane_sum(1)
    for first in range(2):
        plane, low = env_target(first)
        live = jnp.logical_or(z > 0, first == 0)

        @pl.when(jnp.logical_and(live, plane == z))
        def _():
            above[1] = above_s[first]

        @pl.when(jnp.logical_and(live, plane != z))
        def _():
            env_copy(first).start()

    def root_copy(m):
        t = lax.rem(me + m, total)
        return remote(
            gram_s.at[1], root.at[:, mine, :], root_s.at[m], root_r.at[j], t // bonds, lax.rem(t, bonds)
        )

    @pl.when(z == 1)
    def _():
        grow_up()
        gram(1, all_up)
        root[:, mine, :] = gram_s[1]
        loop(1, total, lambda m: root_copy(m).start())

    @pl.when((nodes + z) // 2 != z)
    def _():
        env_wait(1)

    down(0, all_low, above[1])
    ours = plane_sum(0)
    for first in range(2):
        for k in range(ops):
            leaf_out[0, k, first] = ours[first, k]

    def root_wait(i):
        @pl.when(bonds + i != me)
        def _():
            remote(
                gram_s.at[1], root.at[:, pl.ds(pl.multiple_of(i * rows, rows), rows), :],
                root_s.at[0], root_r.at[i], z, twin,
            ).wait_recv()

    loop(0, bonds, root_wait)
    root_out[...] = root[...]

    gather_sent(0, all_low)
    gather_sent(1, all_up)
    loop(1, nodes, lambda m: swap(m).wait_send())
    child_sent(0, nodes + z)

    @pl.when(z > 1)
    def _():
        child_sent(1, z)

    for g in range(2):
        loop(1, bonds, lambda m: sum_copy(g, m).wait_send())
    for first in range(2):
        plane, low = env_target(first)

        @pl.when(jnp.logical_and(jnp.logical_or(z > 0, first == 0), plane != z))
        def _():
            env_copy(first).wait_send()

    @pl.when(z == 1)
    def _():
        loop(1, total, lambda m: root_copy(m).wait_send())


def solution(mesh):
    nodes, bonds = mesh.shape["node"], mesh.shape["bond"]

    def local(bottom, upper, leaf, outside, top):
        rows, width = bottom.shape[1], bottom.shape[2]
        ops = leaf.shape[1]
        dma = pltpu.SemaphoreType.DMA
        return pl.pallas_call(
            functools.partial(kernel, nodes, bonds),
            out_shape=(
                jax.ShapeDtypeStruct((1, ops, 2, rows, width), f32),
                jax.ShapeDtypeStruct((ops, width, width), f32),
            ),
            in_specs=[pl.BlockSpec(memory_space=pltpu.VMEM)] * 5,
            out_specs=(pl.BlockSpec(memory_space=pltpu.VMEM),) * 2,
            scratch_shapes=[
                pltpu.VMEM((bonds * rows * width, width), f32),
                pltpu.VMEM((bonds * rows * width, width), f32),
                pltpu.VMEM((rows, width, width), f32),
                pltpu.VMEM((width * ops * rows, width), f32),
                pltpu.VMEM((width * ops * rows, width), f32),
                pltpu.VMEM((2, ops, rows * width, 2 * width), jnp.bfloat16),
                pltpu.VMEM((2, ops, 2 * width, rows * width), jnp.bfloat16),
                pltpu.VMEM((2 * width, rows * width), jnp.bfloat16),
                pltpu.VMEM((rows * width, 2 * width), jnp.bfloat16),
                pltpu.VMEM((2, ops, width, width), f32),
                pltpu.VMEM((2, ops, rows, width), f32),
                pltpu.VMEM((2, 2, ops, width, width), f32),
                pltpu.VMEM((2, bonds, 2, ops, rows, width), f32),
                pltpu.VMEM((2, ops, rows, width), f32),
                pltpu.VMEM((2, ops, rows, width), f32),
                pltpu.VMEM((ops, width, width), f32),
                dma((2, bonds // 2)),
                dma((2, bonds // 2)),
                dma((2, bonds)),
                dma((nodes,)),
                dma((nodes,)),
                dma((2, bonds)),
                dma((2, bonds)),
                dma((2, bonds)),
                dma((2, bonds)),
                dma((2,)),
                dma((2,)),
                dma((nodes * bonds,)),
                dma((bonds,)),
            ],
            compiler_params=pltpu.CompilerParams(
                collective_id=0, has_side_effects=True, vmem_limit_bytes=56 * 1024 * 1024
            ),
        )(bottom, upper, leaf, outside, top)

    placed = (
        P("node", "bond", None, None),
        P(None, "bond", "node", None),
        P("node", None, None, None, None),
        P(),
        P(),
    )
    return jax.shard_map(
        local,
        mesh=mesh,
        in_specs=placed,
        out_specs=(P("node", None, None, "bond", None), P()),
        check_vma=False,
    )
```

```python
import functools

import jax
import jax.numpy as jnp
from jax import lax
from jax.experimental import pallas as pl
from jax.experimental.pallas import tpu as pltpu
from jax.sharding import PartitionSpec as P

MESH = pl.DeviceIdType.MESH
NN = (((1,), (0,)), ((), ()))
NT = (((1,), (1,)), ((), ()))
f32 = jnp.float32


def split(x):
    high = x.astype(jnp.bfloat16)
    return high, (x - high.astype(f32)).astype(jnp.bfloat16)


def dot(a, b, dims=NN):
    return lax.dot_general(a, b, dims, preferred_element_type=f32)


def wide(x):
    return jnp.concatenate(split(x), axis=1)


def twice(x):
    w = wide(x)
    return jnp.concatenate([w, w], axis=0)


def halves(out):
    half = out.shape[1] // 2
    return out[:, :half] + out[:, half:]


def quarters(out):
    half = out.shape[0] // 2
    return halves(out[:half] + out[half:])


def loop(start, stop, body):
    def step(i, carry):
        body(i)
        return carry

    lax.fori_loop(start, stop, step, 0)


def kernel(
    nodes, bonds,
    bottom, upper, leaf, outside, top,
    leaf_out, root_out,
    all_low, all_up, own_up, grown, worked, side_r, side_l, long_l, long_r, childs, gram_s, part, got, above, above_s, root,
    far_s, near_s, half_s, half_r, piece_r, swap_s, swap_r, child_s, child_r, sum_s, sum_r, env_s, env_r, root_s, root_r,
):
    z, j = lax.axis_index("node"), lax.axis_index("bond")
    me = z * bonds + j
    total = nodes * bonds
    chips = bonds // 2
    twin = j + 1 - 2 * lax.rem(j, 2)
    rows, width = bottom.shape[1], bottom.shape[2]
    ops = leaf.shape[1]
    cols = upper.shape[2]
    block = rows * width
    packed = ops * rows
    mine = pl.ds(pl.multiple_of(j * rows, rows), rows)

    def remote(src, dst, send, recv, plane, bond):
        return pltpu.make_async_remote_copy(
            src_ref=src, dst_ref=dst, send_sem=send, recv_sem=recv,
            device_id=(plane, bond), device_id_type=MESH,
        )

    barrier = pltpu.get_barrier_semaphore()

    def greet(m):
        t = lax.rem(me + m, total)
        pl.semaphore_signal(barrier, inc=1, device_id=(t // bonds, lax.rem(t, bonds)), device_id_type=MESH)

    loop(1, total, greet)

    def turn(src, dst):
        def one(p):
            dst[pl.ds(j * block + p, width, stride=rows), :] = src[p]

        loop(0, rows, one)

    turn(bottom.at[0], all_low)
    pl.semaphore_wait(barrier, total - 1)

    square = chips == 4
    by_x = j + 2 - 4 * lax.rem(j // 2, 2)
    turn_y = 4 - 8 * lax.rem(j // 4, 2)
    by_y, by_xy = j + turn_y, by_x + turn_y

    def piece(whole, i, half=None):
        if half is None:
            return whole.at[pl.ds(pl.multiple_of(i * block, block), block), :]
        size = block // 2
        return whole.at[pl.ds(pl.multiple_of(i * block + half * size, size), size), :]

    def far_copy(g, whole, m, to):
        return remote(piece(whole, j), piece(whole, j), far_s.at[g, m], piece_r.at[g, j], z, to)

    def near_copy(g, whole, i):
        return remote(piece(whole, i), piece(whole, i), near_s.at[g, i // 2], piece_r.at[g, i], z, twin)

    def half_copy(g, whole, i, half, to):
        return remote(
            piece(whole, i, half), piece(whole, i, half), half_s.at[g, half], half_r.at[g, half], z, to
        )

    def arrived(g, whole, i):
        remote(piece(whole, i), piece(whole, i), far_s.at[g, 0], piece_r.at[g, i], z, twin).wait_recv()

    def each_far(act):
        if square:
            act(1, by_x)
            act(2, by_y)
        else:
            loop(1, chips, lambda m: act(m, lax.rem(j + 2 * m, bonds)))

    def gather_start(g, whole):
        each_far(lambda m, to: far_copy(g, whole, m, to).start())
        near_copy(g, whole, j).start()

    def gather_pass(g, whole):
        def one(m, i):
            arrived(g, whole, i)
            if square:
                half_copy(g, whole, i, m - 1, by_y if m == 1 else by_x).start()
            near_copy(g, whole, i).start()

        each_far(one)

    def gather_last(g, whole):
        if square:
            for half in range(2):
                half_copy(g, whole, by_xy, half, twin).wait_recv()
            near_copy(g, whole, by_xy).start()

    def gather_end(g, whole):
        loop(0, chips, lambda m: arrived(g, whole, lax.rem(twin + 2 * m, bonds)))

    def gather_sent(g, whole):
        each_far(lambda m, to: far_copy(g, whole, m, to).wait_send())
        if square:
            half_copy(g, whole, by_x, 0, by_y).wait_send()
            half_copy(g, whole, by_y, 1, by_x).wait_send()
        loop(0, chips, lambda m: near_copy(g, whole, lax.rem(j + 2 * m, bonds)).wait_send())

    gather_start(0, all_low)

    def swap(m):
        t = lax.rem(z + m, nodes)
        return remote(
            upper.at[t], own_up.at[:, pl.ds(pl.multiple_of(z * cols, cols), cols), :],
            swap_s.at[m], swap_r.at[z], t, j,
        )

    loop(1, nodes, lambda m: swap(m).start())

    def keep(p):
        own_up[p, pl.ds(pl.multiple_of(z * cols, cols), cols), :] = upper[z, p]

    loop(0, rows, keep)

    def grow(x_of, left_of, right_of):
        lefts = wide(jnp.concatenate([left_of(k).T for k in range(ops)], axis=0))

        def one(p, carry):
            out = halves(dot(lefts, twice(x_of(p))))
            for k in range(ops):
                grown[pl.ds(k * block + p, width, stride=rows), :] = out[k * width : (k + 1) * width]
            return carry

        lax.fori_loop(0, rows, one, 0, unroll=2)
        step = 4 * width
        for k in range(ops):
            right = twice(right_of(k))

            def chunk(i, carry):
                at = pl.ds(pl.multiple_of(k * block + i * step, step), step)
                grown[at, :] = halves(dot(wide(grown[at, :]), right))
                return carry

            lax.fori_loop(0, block // step, chunk, 0)

    def sides(g, x_of, left_of, right_of):
        rights = wide(jnp.concatenate([right_of(k).T for k in range(ops)], axis=0))

        def one(p, carry):
            turned = x_of(p).T
            out = halves(dot(rights, twice(turned)))
            turned_wide = wide(turned)
            at = pl.ds(pl.multiple_of(p * width, width), width)
            for k in range(ops):
                side_r[g, k, at, :] = wide(out[k * width : (k + 1) * width])
                high, low = split(halves(dot(turned_wide, twice(left_of(k)))))
                side_l[g, k, :width, at] = high
                side_l[g, k, width:, at] = low
            return carry

        lax.fori_loop(0, rows, one, 0, unroll=2)

    def column(whole, c):
        parts = [whole[pl.ds(pl.multiple_of(i * block + c * rows, rows), rows), :] for i in range(bonds)]
        return jnp.concatenate(parts, axis=0)

    def gram(g, whole):
        def slab(c):
            parts = [
                grown[pl.ds(pl.multiple_of(k * block + c * rows, rows), rows), :] for k in range(ops)
            ]
            return jnp.concatenate(split(jnp.concatenate(parts, axis=0)), axis=0)

        def one(i, acc):
            t = jnp.concatenate([slab(2 * i), slab(2 * i + 1)], axis=1)
            x = jnp.concatenate(
                [jnp.concatenate(split(column(whole, 2 * i + d)), axis=0) for d in range(2)], axis=1
            )
            return acc + dot(t, x, NT)

        zero = jnp.zeros((2 * packed, 2 * width), f32)
        out = lax.fori_loop(0, width // 2, one, zero, unroll=4)
        gram_s[g] = quarters(out).reshape(ops, rows, width)

    def sum_copy(g, k, m):
        i = lax.rem(j + m, bonds)
        return remote(
            part.at[g, k, :, pl.ds(pl.multiple_of(i * rows, rows), rows), :], got.at[g, k, j],
            sum_s.at[g, k, m], sum_r.at[g, k, j], z, i,
        )

    def plane_sum(g, k):
        def add(m, acc):
            i = lax.rem(j + m, bonds)
            remote(
                part.at[g, k, :, mine, :], got.at[g, k, i], sum_s.at[g, k, 0], sum_r.at[g, k, i], z, twin
            ).wait_recv()
            return acc + got[g, k, i]

        return lax.fori_loop(1, bonds, add, part[g, k, :, mine, :])

    def down(g, whole, env):
        e = jnp.concatenate(split(env.reshape(packed, width)), axis=0)

        def one(c, carry):
            at = pl.ds(pl.multiple_of(c * packed, packed), packed)
            worked[at, :] = quarters(dot(e, wide(column(whole, c))))
            return carry

        lax.fori_loop(0, width, one, 0, unroll=8)

        def operator(k):
            def fill(p, carry):
                high, low = split(worked[pl.ds(k * rows + p, width, stride=packed), :])
                at = pl.ds(pl.multiple_of(p * width, width), width)
                long_l[:width, at] = high
                long_l[width:, at] = low
                long_r[at, :width] = high
                long_r[at, width:] = low
                return carry

            lax.fori_loop(0, rows, fill, 0, unroll=4)
            part[g, k, 0] = quarters(dot(long_l[...], side_r[g, k])).T
            part[g, k, 1] = quarters(dot(side_l[g, k], long_r[...]))
            loop(1, bonds, lambda m: sum_copy(g, k, m).start())

        loop(0, ops, operator)

    def child_copy(g, number, i):
        return remote(
            gram_s.at[g], childs.at[lax.rem(number, 2), :, mine, :],
            child_s.at[g, i], child_r.at[lax.rem(number, 2), j], number // 2, i,
        )

    def child_send(g, number):
        def one(i):
            own = (number // 2) * bonds + i == me

            @pl.when(own)
            def _():
                childs[lax.rem(number, 2), :, mine, :] = gram_s[g]

            @pl.when(jnp.logical_not(own))
            def _():
                child_copy(g, number, i).start()

        loop(0, bonds, one)

    def child_sent(g, number):
        def one(i):
            @pl.when((number // 2) * bonds + i != me)
            def _():
                child_copy(g, number, i).wait_send()

        loop(0, bonds, one)

    def child_wait():
        for first in range(2):
            number = 2 * z + first
            plane = jnp.where(number >= nodes, number - nodes, number)

            def one(i):
                @pl.when(plane * bonds + i != me)
                def _():
                    remote(
                        gram_s.at[0], childs.at[first, :, pl.ds(pl.multiple_of(i * rows, rows), rows), :],
                        child_s.at[0, 0], child_r.at[first, i], z, twin,
                    ).wait_recv()

            loop(0, bonds, one)

    def env_target(first):
        number = jnp.where(z == 0, 1, 2 * z + first)
        low = (number >= nodes).astype(jnp.int32)
        return number - low * nodes, low

    def env_copy(first):
        plane, low = env_target(first)
        return remote(above_s.at[first], above.at[low], env_s.at[first], env_r.at[low], plane, j)

    def env_wait(low):
        remote(above_s.at[0], above.at[low], env_s.at[0], env_r.at[low], z, twin).wait_recv()

    grow(lambda p: bottom[0, p], lambda k: leaf[0, k, 0], lambda k: leaf[0, k, 1])
    sides(0, lambda p: bottom[0, p], lambda k: leaf[0, k, 0], lambda k: leaf[0, k, 1])

    gather_pass(0, all_low)

    def swapped(m):
        i = lax.rem(z + m, nodes)
        remote(
            upper.at[0], own_up.at[:, pl.ds(pl.multiple_of(i * cols, cols), cols), :],
            swap_s.at[0], swap_r.at[i], lax.rem(z + 1, nodes), j,
        ).wait_recv()

    loop(1, nodes, swapped)
    turn(own_up, all_up)
    gather_last(0, all_low)
    gather_start(1, all_up)
    gather_end(0, all_low)
    gram(0, all_low)
    child_send(0, nodes + z)

    def grow_up():
        grow(lambda p: own_up[p], lambda k: childs[0, k], lambda k: childs[1, k])

    def sides_up():
        sides(1, lambda p: own_up[p], lambda k: childs[0, k], lambda k: childs[1, k])

    gather_pass(1, all_up)

    @pl.when(z == 0)
    def _():
        childs[0] = outside[...]
        childs[1] = outside[...]
        above[0] = top[:, mine, :]
        sides_up()

    @pl.when(z > 1)
    def _():
        child_wait()
        grow_up()

    gather_last(1, all_up)
    gather_end(1, all_up)

    @pl.when(z > 1)
    def _():
        gram(1, all_up)
        child_send(1, z)

    @pl.when(z == 1)
    def _():
        child_wait()

    @pl.when(z > 0)
    def _():
        sides_up()
        env_wait(0)

    down(1, all_up, above[0])
    for k in range(ops):
        above_s[:, k] = plane_sum(1, k)
    for first in range(2):
        plane, low = env_target(first)
        live = jnp.logical_or(z > 0, first == 0)

        @pl.when(jnp.logical_and(live, plane == z))
        def _():
            above[1] = above_s[first]

        @pl.when(jnp.logical_and(live, plane != z))
        def _():
            env_copy(first).start()

    def root_copy(m):
        t = lax.rem(me + m, total)
        return remote(
            gram_s.at[1], root.at[:, mine, :], root_s.at[m], root_r.at[j], t // bonds, lax.rem(t, bonds)
        )

    @pl.when(z == 1)
    def _():
        grow_up()
        gram(1, all_up)
        root[:, mine, :] = gram_s[1]
        loop(1, total, lambda m: root_copy(m).start())

    @pl.when((nodes + z) // 2 != z)
    def _():
        env_wait(1)

    down(0, all_low, above[1])
    for k in range(ops):
        leaf_out[0, k] = plane_sum(0, k)

    def root_wait(i):
        @pl.when(bonds + i != me)
        def _():
            remote(
                gram_s.at[1], root.at[:, pl.ds(pl.multiple_of(i * rows, rows), rows), :],
                root_s.at[0], root_r.at[i], z, twin,
            ).wait_recv()

    loop(0, bonds, root_wait)
    root_out[...] = root[...]

    gather_sent(0, all_low)
    gather_sent(1, all_up)
    loop(1, nodes, lambda m: swap(m).wait_send())
    child_sent(0, nodes + z)

    @pl.when(z > 1)
    def _():
        child_sent(1, z)

    for g in range(2):
        for k in range(ops):
            loop(1, bonds, lambda m: sum_copy(g, k, m).wait_send())
    for first in range(2):
        plane, low = env_target(first)

        @pl.when(jnp.logical_and(jnp.logical_or(z > 0, first == 0), plane != z))
        def _():
            env_copy(first).wait_send()

    @pl.when(z == 1)
    def _():
        loop(1, total, lambda m: root_copy(m).wait_send())


def solution(mesh):
    nodes, bonds = mesh.shape["node"], mesh.shape["bond"]

    def local(bottom, upper, leaf, outside, top):
        rows, width = bottom.shape[1], bottom.shape[2]
        ops = leaf.shape[1]
        dma = pltpu.SemaphoreType.DMA
        return pl.pallas_call(
            functools.partial(kernel, nodes, bonds),
            out_shape=(
                jax.ShapeDtypeStruct((1, ops, 2, rows, width), f32),
                jax.ShapeDtypeStruct((ops, width, width), f32),
            ),
            in_specs=[pl.BlockSpec(memory_space=pltpu.VMEM)] * 5,
            out_specs=(pl.BlockSpec(memory_space=pltpu.VMEM),) * 2,
            scratch_shapes=[
                pltpu.VMEM((bonds * rows * width, width), f32),
                pltpu.VMEM((bonds * rows * width, width), f32),
                pltpu.VMEM((rows, width, width), f32),
                pltpu.VMEM((width * ops * rows, width), f32),
                pltpu.VMEM((width * ops * rows, width), f32),
                pltpu.VMEM((2, ops, rows * width, 2 * width), jnp.bfloat16),
                pltpu.VMEM((2, ops, 2 * width, rows * width), jnp.bfloat16),
                pltpu.VMEM((2 * width, rows * width), jnp.bfloat16),
                pltpu.VMEM((rows * width, 2 * width), jnp.bfloat16),
                pltpu.VMEM((2, ops, width, width), f32),
                pltpu.VMEM((2, ops, rows, width), f32),
                pltpu.VMEM((2, ops, 2, width, width), f32),
                pltpu.VMEM((2, ops, bonds, 2, rows, width), f32),
                pltpu.VMEM((2, ops, rows, width), f32),
                pltpu.VMEM((2, ops, rows, width), f32),
                pltpu.VMEM((ops, width, width), f32),
                dma((2, bonds // 2)),
                dma((2, bonds // 2)),
                dma((2, 2)),
                dma((2, 2)),
                dma((2, bonds)),
                dma((nodes,)),
                dma((nodes,)),
                dma((2, bonds)),
                dma((2, bonds)),
                dma((2, ops, bonds)),
                dma((2, ops, bonds)),
                dma((2,)),
                dma((2,)),
                dma((nodes * bonds,)),
                dma((bonds,)),
            ],
            compiler_params=pltpu.CompilerParams(
                collective_id=0, has_side_effects=True, vmem_limit_bytes=56 * 1024 * 1024
            ),
        )(bottom, upper, leaf, outside, top)

    placed = (
        P("node", "bond", None, None),
        P(None, "bond", "node", None),
        P("node", None, None, None, None),
        P(),
        P(),
    )
    return jax.shard_map(
        local,
        mesh=mesh,
        in_specs=placed,
        out_specs=(P("node", None, None, "bond", None), P()),
        check_vma=False,
    )
```

```python
import functools

import jax
import jax.numpy as jnp
from jax import lax
from jax.experimental import pallas as pl
from jax.experimental.pallas import tpu as pltpu
from jax.sharding import PartitionSpec as P

MESH = pl.DeviceIdType.MESH
NN = (((1,), (0,)), ((), ()))
NT = (((1,), (1,)), ((), ()))
f32 = jnp.float32


def split(x):
    high = x.astype(jnp.bfloat16)
    return high, (x - high.astype(f32)).astype(jnp.bfloat16)


def dot(a, b, dims=NN):
    return lax.dot_general(a, b, dims, preferred_element_type=f32)


def wide(x):
    return jnp.concatenate(split(x), axis=1)


def twice(x):
    w = wide(x)
    return jnp.concatenate([w, w], axis=0)


def halves(out):
    half = out.shape[1] // 2
    return out[:, :half] + out[:, half:]


def quarters(out):
    half = out.shape[0] // 2
    return halves(out[:half] + out[half:])


def loop(start, stop, body):
    def step(i, carry):
        body(i)
        return carry

    lax.fori_loop(start, stop, step, 0)


def kernel(
    nodes, bonds,
    bottom, upper, leaf, outside, top,
    leaf_out, root_out,
    all_low, all_up, own_up, grown, worked, side_r, side_l, long_l, long_r, childs, gram_s, part, got, parts_in, above, root,
    far_s, near_s, half_s, half_r, piece_r, swap_s, swap_r, child_s, child_r, sum_s, sum_r, env_s, env_r, root_s, root_r,
):
    z, j = lax.axis_index("node"), lax.axis_index("bond")
    me = z * bonds + j
    total = nodes * bonds
    chips = bonds // 2
    twin = j + 1 - 2 * lax.rem(j, 2)
    rows, width = bottom.shape[1], bottom.shape[2]
    ops = leaf.shape[1]
    cols = upper.shape[2]
    block = rows * width
    packed = ops * rows
    mine = pl.ds(pl.multiple_of(j * rows, rows), rows)

    def remote(src, dst, send, recv, plane, bond):
        return pltpu.make_async_remote_copy(
            src_ref=src, dst_ref=dst, send_sem=send, recv_sem=recv,
            device_id=(plane, bond), device_id_type=MESH,
        )

    barrier = pltpu.get_barrier_semaphore()

    def greet(m):
        t = lax.rem(me + m, total)
        pl.semaphore_signal(barrier, inc=1, device_id=(t // bonds, lax.rem(t, bonds)), device_id_type=MESH)

    loop(1, total, greet)

    def turn(src, dst):
        def one(p):
            dst[pl.ds(j * block + p, width, stride=rows), :] = src[p]

        loop(0, rows, one)

    turn(bottom.at[0], all_low)
    pl.semaphore_wait(barrier, total - 1)

    square = chips == 4
    by_x = j + 2 - 4 * lax.rem(j // 2, 2)
    turn_y = 4 - 8 * lax.rem(j // 4, 2)
    by_y, by_xy = j + turn_y, by_x + turn_y

    def piece(whole, i, half=None):
        if half is None:
            return whole.at[pl.ds(pl.multiple_of(i * block, block), block), :]
        size = block // 2
        return whole.at[pl.ds(pl.multiple_of(i * block + half * size, size), size), :]

    def far_copy(g, whole, m, to):
        return remote(piece(whole, j), piece(whole, j), far_s.at[g, m], piece_r.at[g, j], z, to)

    def near_copy(g, whole, i):
        return remote(piece(whole, i), piece(whole, i), near_s.at[g, i // 2], piece_r.at[g, i], z, twin)

    def half_copy(g, whole, i, half, to):
        return remote(
            piece(whole, i, half), piece(whole, i, half), half_s.at[g, half], half_r.at[g, half], z, to
        )

    def arrived(g, whole, i):
        remote(piece(whole, i), piece(whole, i), far_s.at[g, 0], piece_r.at[g, i], z, twin).wait_recv()

    def each_far(act):
        if square:
            act(1, by_x)
            act(2, by_y)
        else:
            loop(1, chips, lambda m: act(m, lax.rem(j + 2 * m, bonds)))

    def gather_start(g, whole):
        each_far(lambda m, to: far_copy(g, whole, m, to).start())
        near_copy(g, whole, j).start()

    def gather_pass(g, whole):
        def one(m, i):
            arrived(g, whole, i)
            if square:
                half_copy(g, whole, i, m - 1, by_y if m == 1 else by_x).start()
            near_copy(g, whole, i).start()

        each_far(one)

    def gather_last(g, whole):
        if square:
            for half in range(2):
                half_copy(g, whole, by_xy, half, twin).wait_recv()
            near_copy(g, whole, by_xy).start()

    def gather_end(g, whole):
        loop(0, chips, lambda m: arrived(g, whole, lax.rem(twin + 2 * m, bonds)))

    def gather_sent(g, whole):
        each_far(lambda m, to: far_copy(g, whole, m, to).wait_send())
        if square:
            half_copy(g, whole, by_x, 0, by_y).wait_send()
            half_copy(g, whole, by_y, 1, by_x).wait_send()
        loop(0, chips, lambda m: near_copy(g, whole, lax.rem(j + 2 * m, bonds)).wait_send())

    gather_start(0, all_low)

    def swap(m):
        t = lax.rem(z + m, nodes)
        return remote(
            upper.at[t], own_up.at[:, pl.ds(pl.multiple_of(z * cols, cols), cols), :],
            swap_s.at[m], swap_r.at[z], t, j,
        )

    loop(1, nodes, lambda m: swap(m).start())

    def keep(p):
        own_up[p, pl.ds(pl.multiple_of(z * cols, cols), cols), :] = upper[z, p]

    loop(0, rows, keep)

    def grow(x_of, left_of, right_of):
        lefts = wide(jnp.concatenate([left_of(k).T for k in range(ops)], axis=0))

        def one(p, carry):
            out = halves(dot(lefts, twice(x_of(p))))
            for k in range(ops):
                grown[pl.ds(k * block + p, width, stride=rows), :] = out[k * width : (k + 1) * width]
            return carry

        lax.fori_loop(0, rows, one, 0, unroll=2)
        step = 4 * width
        for k in range(ops):
            right = twice(right_of(k))

            def chunk(i, carry):
                at = pl.ds(pl.multiple_of(k * block + i * step, step), step)
                grown[at, :] = halves(dot(wide(grown[at, :]), right))
                return carry

            lax.fori_loop(0, block // step, chunk, 0)

    def sides(g, x_of, left_of, right_of):
        rights = wide(jnp.concatenate([right_of(k).T for k in range(ops)], axis=0))

        def one(p, carry):
            turned = x_of(p).T
            out = halves(dot(rights, twice(turned)))
            turned_wide = wide(turned)
            at = pl.ds(pl.multiple_of(p * width, width), width)
            for k in range(ops):
                side_r[g, k, at, :] = wide(out[k * width : (k + 1) * width])
                high, low = split(halves(dot(turned_wide, twice(left_of(k)))))
                side_l[g, k, :width, at] = high
                side_l[g, k, width:, at] = low
            return carry

        lax.fori_loop(0, rows, one, 0, unroll=2)

    def column(whole, c):
        parts = [whole[pl.ds(pl.multiple_of(i * block + c * rows, rows), rows), :] for i in range(bonds)]
        return jnp.concatenate(parts, axis=0)

    def gram(g, whole):
        def slab(c):
            parts = [
                grown[pl.ds(pl.multiple_of(k * block + c * rows, rows), rows), :] for k in range(ops)
            ]
            return jnp.concatenate(split(jnp.concatenate(parts, axis=0)), axis=0)

        def one(i, acc):
            t = jnp.concatenate([slab(2 * i), slab(2 * i + 1)], axis=1)
            x = jnp.concatenate(
                [jnp.concatenate(split(column(whole, 2 * i + d)), axis=0) for d in range(2)], axis=1
            )
            return acc + dot(t, x, NT)

        zero = jnp.zeros((2 * packed, 2 * width), f32)
        out = lax.fori_loop(0, width // 2, one, zero, unroll=4)
        gram_s[g] = quarters(out).reshape(ops, rows, width)

    def band(i):
        return pl.ds(pl.multiple_of(i * rows, rows), rows)

    def sum_copy(k, m):
        i = lax.rem(j + m, bonds)
        return remote(
            part.at[0, k, :, band(i), :], got.at[k, j], sum_s.at[k, m], sum_r.at[k, j], z, i
        )

    def plane_sum(k):
        def add(m, acc):
            i = lax.rem(j + m, bonds)
            remote(
                part.at[0, k, :, mine, :], got.at[k, i], sum_s.at[k, 0], sum_r.at[k, i], z, twin
            ).wait_recv()
            return acc + got[k, i]

        return lax.fori_loop(1, bonds, add, part[0, k, :, mine, :])

    def env_target(first):
        number = jnp.where(z == 0, 1, 2 * z + first)
        low = (number >= nodes).astype(jnp.int32)
        return number - low * nodes, low, jnp.logical_or(z > 0, first == 0)

    def env_copy(k, first, i):
        plane, low, _ = env_target(first)
        return remote(
            part.at[1, k, first, band(i), :], parts_in.at[low, k, j],
            env_s.at[first, k, i], env_r.at[low, k, j], plane, i,
        )

    def env_each(k, act, keep_own):
        for first in range(2):
            plane, low, live = env_target(first)

            def one(i):
                own = plane * bonds + i == me

                @pl.when(jnp.logical_and(live, jnp.logical_not(own)))
                def _():
                    act(env_copy(k, first, i))

                if keep_own:
                    @pl.when(jnp.logical_and(live, own))
                    def _():
                        parts_in[low, k, j] = part[1, k, first, mine, :]

            loop(0, bonds, one)

    def env_send(k):
        env_each(k, lambda copy: copy.start(), True)

    def env_sent(k):
        env_each(k, lambda copy: copy.wait_send(), False)

    def env_wait(low):
        source = (nodes * low + z) // 2

        def operator(k):
            def add(i, acc):
                @pl.when(source * bonds + i != me)
                def _():
                    remote(
                        part.at[1, 0, 0, mine, :], parts_in.at[low, k, i],
                        env_s.at[0, 0, 0], env_r.at[low, k, i], z, twin,
                    ).wait_recv()

                return acc + parts_in[low, k, i]

            above[low, k] = lax.fori_loop(0, bonds, add, jnp.zeros((rows, width), f32))

        loop(0, ops, operator)

    def down(g, whole, env):
        e = jnp.concatenate(split(env.reshape(packed, width)), axis=0)
        e = jnp.concatenate([e, e], axis=1)

        def one(i, carry):
            x = jnp.concatenate(
                [jnp.concatenate(split(column(whole, 2 * i + d)), axis=0) for d in range(2)], axis=1
            )
            out = dot(e, x)
            out = out[:packed] + out[packed:]
            at = pl.multiple_of(2 * i * packed, packed)
            worked[pl.ds(at, packed), :] = out[:, :width]
            worked[pl.ds(at + packed, packed), :] = out[:, width:]
            return carry

        lax.fori_loop(0, width // 2, one, 0, unroll=4)

        def operator(k):
            def fill(p, carry):
                high, low = split(worked[pl.ds(k * rows + p, width, stride=packed), :])
                at = pl.ds(pl.multiple_of(p * width, width), width)
                long_l[:width, at] = high
                long_l[width:, at] = low
                long_r[at, :width] = high
                long_r[at, width:] = low
                return carry

            lax.fori_loop(0, rows, fill, 0, unroll=4)
            part[g, k, 0] = quarters(dot(long_l[...], side_r[g, k])).T
            part[g, k, 1] = quarters(dot(side_l[g, k], long_r[...]))
            if g == 0:
                loop(1, bonds, lambda m: sum_copy(k, m).start())
            else:
                env_send(k)

        loop(0, ops, operator)

    def child_copy(g, number, i):
        return remote(
            gram_s.at[g], childs.at[lax.rem(number, 2), :, mine, :],
            child_s.at[g, i], child_r.at[lax.rem(number, 2), j], number // 2, i,
        )

    def child_send(g, number):
        def one(i):
            own = (number // 2) * bonds + i == me

            @pl.when(own)
            def _():
                childs[lax.rem(number, 2), :, mine, :] = gram_s[g]

            @pl.when(jnp.logical_not(own))
            def _():
                child_copy(g, number, i).start()

        loop(0, bonds, one)

    def child_sent(g, number):
        def one(i):
            @pl.when((number // 2) * bonds + i != me)
            def _():
                child_copy(g, number, i).wait_send()

        loop(0, bonds, one)

    def child_wait():
        for first in range(2):
            number = 2 * z + first
            plane = jnp.where(number >= nodes, number - nodes, number)

            def one(i):
                @pl.when(plane * bonds + i != me)
                def _():
                    remote(
                        gram_s.at[0], childs.at[first, :, pl.ds(pl.multiple_of(i * rows, rows), rows), :],
                        child_s.at[0, 0], child_r.at[first, i], z, twin,
                    ).wait_recv()

            loop(0, bonds, one)

    grow(lambda p: bottom[0, p], lambda k: leaf[0, k, 0], lambda k: leaf[0, k, 1])
    gather_pass(0, all_low)
    sides(0, lambda p: bottom[0, p], lambda k: leaf[0, k, 0], lambda k: leaf[0, k, 1])

    def swapped(m):
        i = lax.rem(z + m, nodes)
        remote(
            upper.at[0], own_up.at[:, pl.ds(pl.multiple_of(i * cols, cols), cols), :],
            swap_s.at[0], swap_r.at[i], lax.rem(z + 1, nodes), j,
        ).wait_recv()

    loop(1, nodes, swapped)
    turn(own_up, all_up)
    gather_last(0, all_low)
    gather_start(1, all_up)
    gather_end(0, all_low)
    gram(0, all_low)
    child_send(0, nodes + z)

    def grow_up():
        grow(lambda p: own_up[p], lambda k: childs[0, k], lambda k: childs[1, k])

    def sides_up():
        sides(1, lambda p: own_up[p], lambda k: childs[0, k], lambda k: childs[1, k])

    gather_pass(1, all_up)

    @pl.when(z == 0)
    def _():
        childs[0] = outside[...]
        childs[1] = outside[...]
        above[0] = top[:, mine, :]
        sides_up()

    @pl.when(z > 1)
    def _():
        child_wait()
        grow_up()

    gather_last(1, all_up)
    gather_end(1, all_up)

    @pl.when(z > 1)
    def _():
        gram(1, all_up)
        child_send(1, z)

    @pl.when(z == 1)
    def _():
        child_wait()

    @pl.when(z > 0)
    def _():
        sides_up()
        env_wait(0)

    down(1, all_up, above[0])
    def root_copy(m):
        t = lax.rem(me + m, total)
        return remote(
            gram_s.at[1], root.at[:, mine, :], root_s.at[m], root_r.at[j], t // bonds, lax.rem(t, bonds)
        )

    @pl.when(z == 1)
    def _():
        grow_up()
        gram(1, all_up)
        root[:, mine, :] = gram_s[1]
        loop(1, total, lambda m: root_copy(m).start())

    env_wait(1)
    down(0, all_low, above[1])
    for k in range(ops):
        leaf_out[0, k] = plane_sum(k)

    def root_wait(i):
        @pl.when(bonds + i != me)
        def _():
            remote(
                gram_s.at[1], root.at[:, pl.ds(pl.multiple_of(i * rows, rows), rows), :],
                root_s.at[0], root_r.at[i], z, twin,
            ).wait_recv()

    loop(0, bonds, root_wait)
    root_out[...] = root[...]

    gather_sent(0, all_low)
    gather_sent(1, all_up)
    loop(1, nodes, lambda m: swap(m).wait_send())
    child_sent(0, nodes + z)

    @pl.when(z > 1)
    def _():
        child_sent(1, z)

    for k in range(ops):
        loop(1, bonds, lambda m: sum_copy(k, m).wait_send())
        env_sent(k)

    @pl.when(z == 1)
    def _():
        loop(1, total, lambda m: root_copy(m).wait_send())


def solution(mesh):
    nodes, bonds = mesh.shape["node"], mesh.shape["bond"]

    def local(bottom, upper, leaf, outside, top):
        rows, width = bottom.shape[1], bottom.shape[2]
        ops = leaf.shape[1]
        dma = pltpu.SemaphoreType.DMA
        return pl.pallas_call(
            functools.partial(kernel, nodes, bonds),
            out_shape=(
                jax.ShapeDtypeStruct((1, ops, 2, rows, width), f32),
                jax.ShapeDtypeStruct((ops, width, width), f32),
            ),
            in_specs=[pl.BlockSpec(memory_space=pltpu.VMEM)] * 5,
            out_specs=(pl.BlockSpec(memory_space=pltpu.VMEM),) * 2,
            scratch_shapes=[
                pltpu.VMEM((bonds * rows * width, width), f32),
                pltpu.VMEM((bonds * rows * width, width), f32),
                pltpu.VMEM((rows, width, width), f32),
                pltpu.VMEM((width * ops * rows, width), f32),
                pltpu.VMEM((width * ops * rows, width), f32),
                pltpu.VMEM((2, ops, rows * width, 2 * width), jnp.bfloat16),
                pltpu.VMEM((2, ops, 2 * width, rows * width), jnp.bfloat16),
                pltpu.VMEM((2 * width, rows * width), jnp.bfloat16),
                pltpu.VMEM((rows * width, 2 * width), jnp.bfloat16),
                pltpu.VMEM((2, ops, width, width), f32),
                pltpu.VMEM((2, ops, rows, width), f32),
                pltpu.VMEM((2, ops, 2, width, width), f32),
                pltpu.VMEM((ops, bonds, 2, rows, width), f32),
                pltpu.VMEM((2, ops, bonds, rows, width), f32),
                pltpu.VMEM((2, ops, rows, width), f32),
                pltpu.VMEM((ops, width, width), f32),
                dma((2, bonds // 2)),
                dma((2, bonds // 2)),
                dma((2, 2)),
                dma((2, 2)),
                dma((2, bonds)),
                dma((nodes,)),
                dma((nodes,)),
                dma((2, bonds)),
                dma((2, bonds)),
                dma((ops, bonds)),
                dma((ops, bonds)),
                dma((2, ops, bonds)),
                dma((2, ops, bonds)),
                dma((nodes * bonds,)),
                dma((bonds,)),
            ],
            compiler_params=pltpu.CompilerParams(
                collective_id=0, has_side_effects=True, vmem_limit_bytes=56 * 1024 * 1024
            ),
        )(bottom, upper, leaf, outside, top)

    placed = (
        P("node", "bond", None, None),
        P(None, "bond", "node", None),
        P("node", None, None, None, None),
        P(),
        P(),
    )
    return jax.shard_map(
        local,
        mesh=mesh,
        in_specs=placed,
        out_specs=(P("node", None, None, "bond", None), P()),
        check_vma=False,
    )
```

```python
import functools

import jax
import jax.numpy as jnp
from jax import lax
from jax.experimental import pallas as pl
from jax.experimental.pallas import tpu as pltpu
from jax.sharding import PartitionSpec as P

MESH = pl.DeviceIdType.MESH
NN = (((1,), (0,)), ((), ()))
NT = (((1,), (1,)), ((), ()))
f32 = jnp.float32


def split(x):
    high = x.astype(jnp.bfloat16)
    return high, (x - high.astype(f32)).astype(jnp.bfloat16)


def dot(a, b, dims=NN):
    return lax.dot_general(a, b, dims, preferred_element_type=f32)


def wide(x):
    return jnp.concatenate(split(x), axis=1)


def twice(x):
    w = wide(x)
    return jnp.concatenate([w, w], axis=0)


def halves(out):
    half = out.shape[1] // 2
    return out[:, :half] + out[:, half:]


def quarters(out):
    half = out.shape[0] // 2
    return halves(out[:half] + out[half:])


def loop(start, stop, body):
    def step(i, carry):
        body(i)
        return carry

    lax.fori_loop(start, stop, step, 0)


def kernel(
    nodes, bonds,
    bottom, upper, leaf, outside, top,
    leaf_out, root_out,
    all_low, all_up, own_up, grown, worked, side_r, side_l, long_l, long_r, childs, gram_s, part, got, parts_in, above, root,
    far_s, near_s, half_s, half_r, piece_r, swap_s, swap_r, child_s, child_r, sum_s, sum_r, env_s, env_r, root_s, root_r,
):
    z, j = lax.axis_index("node"), lax.axis_index("bond")
    me = z * bonds + j
    total = nodes * bonds
    chips = bonds // 2
    twin = j + 1 - 2 * lax.rem(j, 2)
    rows, width = bottom.shape[1], bottom.shape[2]
    ops = leaf.shape[1]
    cols = upper.shape[2]
    block = rows * width
    packed = ops * rows
    mine = pl.ds(pl.multiple_of(j * rows, rows), rows)

    def remote(src, dst, send, recv, plane, bond):
        return pltpu.make_async_remote_copy(
            src_ref=src, dst_ref=dst, send_sem=send, recv_sem=recv,
            device_id=(plane, bond), device_id_type=MESH,
        )

    barrier = pltpu.get_barrier_semaphore()

    def greet(m):
        t = lax.rem(me + m, total)
        pl.semaphore_signal(barrier, inc=1, device_id=(t // bonds, lax.rem(t, bonds)), device_id_type=MESH)

    loop(1, total, greet)

    def turn(src, dst):
        def one(p):
            dst[pl.ds(j * block + p, width, stride=rows), :] = src[p]

        loop(0, rows, one)

    turn(bottom.at[0], all_low)
    pl.semaphore_wait(barrier, total - 1)

    square = chips == 4
    by_x = j + 2 - 4 * lax.rem(j // 2, 2)
    turn_y = 4 - 8 * lax.rem(j // 4, 2)
    by_y, by_xy = j + turn_y, by_x + turn_y

    def piece(whole, i, half=None):
        if half is None:
            return whole.at[pl.ds(pl.multiple_of(i * block, block), block), :]
        size = block // 2
        return whole.at[pl.ds(pl.multiple_of(i * block + half * size, size), size), :]

    def far_copy(g, whole, m, to):
        return remote(piece(whole, j), piece(whole, j), far_s.at[g, m], piece_r.at[g, j], z, to)

    def near_copy(g, whole, i):
        return remote(piece(whole, i), piece(whole, i), near_s.at[g, i // 2], piece_r.at[g, i], z, twin)

    def half_copy(g, whole, i, half, to):
        return remote(
            piece(whole, i, half), piece(whole, i, half), half_s.at[g, half], half_r.at[g, half], z, to
        )

    def arrived(g, whole, i):
        remote(piece(whole, i), piece(whole, i), far_s.at[g, 0], piece_r.at[g, i], z, twin).wait_recv()

    def each_far(act):
        if square:
            act(1, by_x)
            act(2, by_y)
        else:
            loop(1, chips, lambda m: act(m, lax.rem(j + 2 * m, bonds)))

    def gather_start(g, whole):
        each_far(lambda m, to: far_copy(g, whole, m, to).start())
        near_copy(g, whole, j).start()

    def gather_pass(g, whole):
        def one(m, i):
            arrived(g, whole, i)
            if square:
                half_copy(g, whole, i, m - 1, by_y if m == 1 else by_x).start()
            near_copy(g, whole, i).start()

        each_far(one)

    def gather_last(g, whole):
        if square:
            for half in range(2):
                half_copy(g, whole, by_xy, half, twin).wait_recv()
            near_copy(g, whole, by_xy).start()

    def gather_end(g, whole):
        loop(0, chips, lambda m: arrived(g, whole, lax.rem(twin + 2 * m, bonds)))

    def gather_sent(g, whole):
        each_far(lambda m, to: far_copy(g, whole, m, to).wait_send())
        if square:
            half_copy(g, whole, by_x, 0, by_y).wait_send()
            half_copy(g, whole, by_y, 1, by_x).wait_send()
        loop(0, chips, lambda m: near_copy(g, whole, lax.rem(j + 2 * m, bonds)).wait_send())

    gather_start(0, all_low)

    def swap(m):
        t = lax.rem(z + m, nodes)
        return remote(
            upper.at[t], own_up.at[:, pl.ds(pl.multiple_of(z * cols, cols), cols), :],
            swap_s.at[m], swap_r.at[z], t, j,
        )

    loop(1, nodes, lambda m: swap(m).start())

    def keep(p):
        own_up[p, pl.ds(pl.multiple_of(z * cols, cols), cols), :] = upper[z, p]

    loop(0, rows, keep)

    def grow(x_of, left_of, right_of):
        lefts = wide(jnp.concatenate([left_of(k).T for k in range(ops)], axis=0))

        def one(p, carry):
            out = halves(dot(lefts, twice(x_of(p))))
            for k in range(ops):
                grown[pl.ds(k * block + p, width, stride=rows), :] = out[k * width : (k + 1) * width]
            return carry

        lax.fori_loop(0, rows, one, 0, unroll=2)
        step = 4 * width
        for k in range(ops):
            right = twice(right_of(k))

            def chunk(i, carry):
                at = pl.ds(pl.multiple_of(k * block + i * step, step), step)
                grown[at, :] = halves(dot(wide(grown[at, :]), right))
                return carry

            lax.fori_loop(0, block // step, chunk, 0)

    def sides(g, x_of, left_of, right_of):
        rights = wide(jnp.concatenate([right_of(k).T for k in range(ops)], axis=0))

        def one(p, carry):
            turned = x_of(p).T
            out = halves(dot(rights, twice(turned)))
            turned_wide = wide(turned)
            at = pl.ds(pl.multiple_of(p * width, width), width)
            for k in range(ops):
                side_r[g, k, at, :] = wide(out[k * width : (k + 1) * width])
                high, low = split(halves(dot(turned_wide, twice(left_of(k)))))
                side_l[g, k, :width, at] = high
                side_l[g, k, width:, at] = low
            return carry

        lax.fori_loop(0, rows, one, 0, unroll=2)

    def column(whole, c):
        parts = [whole[pl.ds(pl.multiple_of(i * block + c * rows, rows), rows), :] for i in range(bonds)]
        return jnp.concatenate(parts, axis=0)

    def gram(g, whole):
        def slab(c):
            parts = [
                grown[pl.ds(pl.multiple_of(k * block + c * rows, rows), rows), :] for k in range(ops)
            ]
            return jnp.concatenate(split(jnp.concatenate(parts, axis=0)), axis=0)

        def one(i, acc):
            t = jnp.concatenate([slab(2 * i), slab(2 * i + 1)], axis=1)
            x = jnp.concatenate(
                [jnp.concatenate(split(column(whole, 2 * i + d)), axis=0) for d in range(2)], axis=1
            )
            return acc + dot(t, x, NT)

        zero = jnp.zeros((2 * packed, 2 * width), f32)
        out = lax.fori_loop(0, width // 2, one, zero, unroll=16)
        gram_s[g] = quarters(out).reshape(ops, rows, width)

    def band(i):
        return pl.ds(pl.multiple_of(i * rows, rows), rows)

    def sum_copy(k, m):
        i = lax.rem(j + m, bonds)
        return remote(
            part.at[0, k, :, band(i), :], got.at[k, j], sum_s.at[k, m], sum_r.at[k, j], z, i
        )

    def plane_sum(k):
        def add(m, acc):
            i = lax.rem(j + m, bonds)
            remote(
                part.at[0, k, :, mine, :], got.at[k, i], sum_s.at[k, 0], sum_r.at[k, i], z, twin
            ).wait_recv()
            return acc + got[k, i]

        return lax.fori_loop(1, bonds, add, part[0, k, :, mine, :])

    def env_target(first):
        number = jnp.where(z == 0, 1, 2 * z + first)
        low = (number >= nodes).astype(jnp.int32)
        return number - low * nodes, low, jnp.logical_or(z > 0, first == 0)

    def env_copy(k, first, i):
        plane, low, _ = env_target(first)
        return remote(
            part.at[1, k, first, band(i), :], parts_in.at[low, k, j],
            env_s.at[first, k, i], env_r.at[low, k, j], plane, i,
        )

    def env_each(k, act, keep_own):
        for first in range(2):
            plane, low, live = env_target(first)

            def one(i):
                own = plane * bonds + i == me

                @pl.when(jnp.logical_and(live, jnp.logical_not(own)))
                def _():
                    act(env_copy(k, first, i))

                if keep_own:
                    @pl.when(jnp.logical_and(live, own))
                    def _():
                        parts_in[low, k, j] = part[1, k, first, mine, :]

            loop(0, bonds, one)

    def env_send(k):
        env_each(k, lambda copy: copy.start(), True)

    def env_sent(k):
        env_each(k, lambda copy: copy.wait_send(), False)

    def env_wait(low):
        source = (nodes * low + z) // 2

        def operator(k):
            def add(i, acc):
                @pl.when(source * bonds + i != me)
                def _():
                    remote(
                        part.at[1, 0, 0, mine, :], parts_in.at[low, k, i],
                        env_s.at[0, 0, 0], env_r.at[low, k, i], z, twin,
                    ).wait_recv()

                return acc + parts_in[low, k, i]

            above[low, k] = lax.fori_loop(0, bonds, add, jnp.zeros((rows, width), f32))

        loop(0, ops, operator)

    def down(g, whole, env):
        e = jnp.concatenate(split(env.reshape(packed, width)), axis=0)
        e = jnp.concatenate([e, e], axis=1)

        def one(i, carry):
            x = jnp.concatenate(
                [jnp.concatenate(split(column(whole, 2 * i + d)), axis=0) for d in range(2)], axis=1
            )
            out = dot(e, x)
            out = out[:packed] + out[packed:]
            at = pl.multiple_of(2 * i * packed, packed)
            worked[pl.ds(at, packed), :] = out[:, :width]
            worked[pl.ds(at + packed, packed), :] = out[:, width:]
            return carry

        lax.fori_loop(0, width // 2, one, 0, unroll=16)

        def operator(k):
            def fill(p, carry):
                high, low = split(worked[pl.ds(k * rows + p, width, stride=packed), :])
                at = pl.ds(pl.multiple_of(p * width, width), width)
                long_l[:width, at] = high
                long_l[width:, at] = low
                long_r[at, :width] = high
                long_r[at, width:] = low
                return carry

            lax.fori_loop(0, rows, fill, 0, unroll=8)
            part[g, k, 0] = quarters(dot(long_l[...], side_r[g, k])).T
            part[g, k, 1] = quarters(dot(side_l[g, k], long_r[...]))
            if g == 0:
                loop(1, bonds, lambda m: sum_copy(k, m).start())
            else:
                env_send(k)

        loop(0, ops, operator)

    def child_copy(g, number, i):
        return remote(
            gram_s.at[g], childs.at[lax.rem(number, 2), :, mine, :],
            child_s.at[g, i], child_r.at[lax.rem(number, 2), j], number // 2, i,
        )

    def child_send(g, number):
        def one(i):
            own = (number // 2) * bonds + i == me

            @pl.when(own)
            def _():
                childs[lax.rem(number, 2), :, mine, :] = gram_s[g]

            @pl.when(jnp.logical_not(own))
            def _():
                child_copy(g, number, i).start()

        loop(0, bonds, one)

    def child_sent(g, number):
        def one(i):
            @pl.when((number // 2) * bonds + i != me)
            def _():
                child_copy(g, number, i).wait_send()

        loop(0, bonds, one)

    def child_wait():
        for first in range(2):
            number = 2 * z + first
            plane = jnp.where(number >= nodes, number - nodes, number)

            def one(i):
                @pl.when(plane * bonds + i != me)
                def _():
                    remote(
                        gram_s.at[0], childs.at[first, :, pl.ds(pl.multiple_of(i * rows, rows), rows), :],
                        child_s.at[0, 0], child_r.at[first, i], z, twin,
                    ).wait_recv()

            loop(0, bonds, one)

    grow(lambda p: bottom[0, p], lambda k: leaf[0, k, 0], lambda k: leaf[0, k, 1])
    gather_pass(0, all_low)

    def swapped(m):
        i = lax.rem(z + m, nodes)
        remote(
            upper.at[0], own_up.at[:, pl.ds(pl.multiple_of(i * cols, cols), cols), :],
            swap_s.at[0], swap_r.at[i], lax.rem(z + 1, nodes), j,
        ).wait_recv()

    loop(1, nodes, swapped)
    turn(own_up, all_up)
    gather_start(1, all_up)
    sides(0, lambda p: bottom[0, p], lambda k: leaf[0, k, 0], lambda k: leaf[0, k, 1])
    gather_last(0, all_low)
    gather_end(0, all_low)
    gram(0, all_low)
    child_send(0, nodes + z)

    def grow_up():
        grow(lambda p: own_up[p], lambda k: childs[0, k], lambda k: childs[1, k])

    def sides_up():
        sides(1, lambda p: own_up[p], lambda k: childs[0, k], lambda k: childs[1, k])

    gather_pass(1, all_up)

    @pl.when(z == 0)
    def _():
        childs[0] = outside[...]
        childs[1] = outside[...]
        above[0] = top[:, mine, :]
        sides_up()

    @pl.when(z > 1)
    def _():
        child_wait()
        grow_up()

    gather_last(1, all_up)
    gather_end(1, all_up)

    @pl.when(z > 1)
    def _():
        gram(1, all_up)
        child_send(1, z)

    @pl.when(z == 1)
    def _():
        child_wait()

    @pl.when(z > 0)
    def _():
        sides_up()
        env_wait(0)

    down(1, all_up, above[0])
    def root_copy(m):
        t = lax.rem(me + m, total)
        return remote(
            gram_s.at[1], root.at[:, mine, :], root_s.at[m], root_r.at[j], t // bonds, lax.rem(t, bonds)
        )

    @pl.when(z == 1)
    def _():
        grow_up()
        gram(1, all_up)
        root[:, mine, :] = gram_s[1]
        loop(1, total, lambda m: root_copy(m).start())

    env_wait(1)
    down(0, all_low, above[1])
    for k in range(ops):
        leaf_out[0, k] = plane_sum(k)

    def root_wait(i):
        @pl.when(bonds + i != me)
        def _():
            remote(
                gram_s.at[1], root.at[:, pl.ds(pl.multiple_of(i * rows, rows), rows), :],
                root_s.at[0], root_r.at[i], z, twin,
            ).wait_recv()

    loop(0, bonds, root_wait)
    root_out[...] = root[...]

    gather_sent(0, all_low)
    gather_sent(1, all_up)
    loop(1, nodes, lambda m: swap(m).wait_send())
    child_sent(0, nodes + z)

    @pl.when(z > 1)
    def _():
        child_sent(1, z)

    for k in range(ops):
        loop(1, bonds, lambda m: sum_copy(k, m).wait_send())
        env_sent(k)

    @pl.when(z == 1)
    def _():
        loop(1, total, lambda m: root_copy(m).wait_send())


def solution(mesh):
    nodes, bonds = mesh.shape["node"], mesh.shape["bond"]

    def local(bottom, upper, leaf, outside, top):
        rows, width = bottom.shape[1], bottom.shape[2]
        ops = leaf.shape[1]
        dma = pltpu.SemaphoreType.DMA
        return pl.pallas_call(
            functools.partial(kernel, nodes, bonds),
            out_shape=(
                jax.ShapeDtypeStruct((1, ops, 2, rows, width), f32),
                jax.ShapeDtypeStruct((ops, width, width), f32),
            ),
            in_specs=[pl.BlockSpec(memory_space=pltpu.VMEM)] * 5,
            out_specs=(pl.BlockSpec(memory_space=pltpu.VMEM),) * 2,
            scratch_shapes=[
                pltpu.VMEM((bonds * rows * width, width), f32),
                pltpu.VMEM((bonds * rows * width, width), f32),
                pltpu.VMEM((rows, width, width), f32),
                pltpu.VMEM((width * ops * rows, width), f32),
                pltpu.VMEM((width * ops * rows, width), f32),
                pltpu.VMEM((2, ops, rows * width, 2 * width), jnp.bfloat16),
                pltpu.VMEM((2, ops, 2 * width, rows * width), jnp.bfloat16),
                pltpu.VMEM((2 * width, rows * width), jnp.bfloat16),
                pltpu.VMEM((rows * width, 2 * width), jnp.bfloat16),
                pltpu.VMEM((2, ops, width, width), f32),
                pltpu.VMEM((2, ops, rows, width), f32),
                pltpu.VMEM((2, ops, 2, width, width), f32),
                pltpu.VMEM((ops, bonds, 2, rows, width), f32),
                pltpu.VMEM((2, ops, bonds, rows, width), f32),
                pltpu.VMEM((2, ops, rows, width), f32),
                pltpu.VMEM((ops, width, width), f32),
                dma((2, bonds // 2)),
                dma((2, bonds // 2)),
                dma((2, 2)),
                dma((2, 2)),
                dma((2, bonds)),
                dma((nodes,)),
                dma((nodes,)),
                dma((2, bonds)),
                dma((2, bonds)),
                dma((ops, bonds)),
                dma((ops, bonds)),
                dma((2, ops, bonds)),
                dma((2, ops, bonds)),
                dma((nodes * bonds,)),
                dma((bonds,)),
            ],
            compiler_params=pltpu.CompilerParams(
                collective_id=0, has_side_effects=True, vmem_limit_bytes=56 * 1024 * 1024
            ),
        )(bottom, upper, leaf, outside, top)

    placed = (
        P("node", "bond", None, None),
        P(None, "bond", "node", None),
        P("node", None, None, None, None),
        P(),
        P(),
    )
    return jax.shard_map(
        local,
        mesh=mesh,
        in_specs=placed,
        out_specs=(P("node", None, None, "bond", None), P()),
        check_vma=False,
    )
```

```python
import functools

import jax
import jax.numpy as jnp
from jax import lax
from jax.experimental import pallas as pl
from jax.experimental.pallas import tpu as pltpu
from jax.sharding import PartitionSpec as P

MESH = pl.DeviceIdType.MESH
NN = (((1,), (0,)), ((), ()))
NT = (((1,), (1,)), ((), ()))
f32 = jnp.float32


def split(x):
    high = x.astype(jnp.bfloat16)
    return high, (x - high.astype(f32)).astype(jnp.bfloat16)


def dot(a, b, dims=NN):
    return lax.dot_general(a, b, dims, preferred_element_type=f32)


def wide(x):
    return jnp.concatenate(split(x), axis=1)


def twice(x):
    w = wide(x)
    return jnp.concatenate([w, w], axis=0)


def halves(out):
    half = out.shape[1] // 2
    return out[:, :half] + out[:, half:]


def quarters(out):
    half = out.shape[0] // 2
    return halves(out[:half] + out[half:])


def loop(start, stop, body):
    def step(i, carry):
        body(i)
        return carry

    lax.fori_loop(start, stop, step, 0)


def kernel(
    nodes, bonds,
    bottom, upper, leaf, outside, top,
    leaf_out, root_out,
    all_low, all_up, own_up, grown, worked, side_r, side_l, long_l, long_r, childs, gram_s, part, got, parts_in, above, root,
    far_s, near_s, half_s, half_r, early_s, early_r, piece_r, swap_s, swap_r, child_s, child_r, sum_s, sum_r, env_s, env_r, root_s, root_r,
):
    z, j = lax.axis_index("node"), lax.axis_index("bond")
    me = z * bonds + j
    total = nodes * bonds
    chips = bonds // 2
    twin = j + 1 - 2 * lax.rem(j, 2)
    rows, width = bottom.shape[1], bottom.shape[2]
    ops = leaf.shape[1]
    cols = upper.shape[2]
    block = rows * width
    packed = ops * rows
    mine = pl.ds(pl.multiple_of(j * rows, rows), rows)

    def remote(src, dst, send, recv, plane, bond):
        return pltpu.make_async_remote_copy(
            src_ref=src, dst_ref=dst, send_sem=send, recv_sem=recv,
            device_id=(plane, bond), device_id_type=MESH,
        )

    barrier = pltpu.get_barrier_semaphore()

    def greet(m):
        t = lax.rem(me + m, total)
        pl.semaphore_signal(barrier, inc=1, device_id=(t // bonds, lax.rem(t, bonds)), device_id_type=MESH)

    loop(1, total, greet)

    def turn(src, dst):
        def one(p):
            dst[pl.ds(j * block + p, width, stride=rows), :] = src[p]

        loop(0, rows, one)

    turn(bottom.at[0], all_low)
    pl.semaphore_wait(barrier, total - 1)

    square = chips == 4
    by_x = j + 2 - 4 * lax.rem(j // 2, 2)
    turn_y = 4 - 8 * lax.rem(j // 4, 2)
    by_y, by_xy = j + turn_y, by_x + turn_y

    def piece(whole, i, half=None):
        if half is None:
            return whole.at[pl.ds(pl.multiple_of(i * block, block), block), :]
        size = block // 2
        return whole.at[pl.ds(pl.multiple_of(i * block + half * size, size), size), :]

    def far_copy(g, whole, m, to):
        return remote(piece(whole, j), piece(whole, j), far_s.at[g, m], piece_r.at[g, j], z, to)

    def near_copy(g, whole, i):
        return remote(piece(whole, i), piece(whole, i), near_s.at[g, i // 2], piece_r.at[g, i], z, twin)

    def half_copy(g, whole, i, half, to):
        return remote(
            piece(whole, i, half), piece(whole, i, half), half_s.at[g, half], half_r.at[g, half], z, to
        )

    def arrived(g, whole, i):
        remote(piece(whole, i), piece(whole, i), far_s.at[g, 0], piece_r.at[g, i], z, twin).wait_recv()

    def each_far(act):
        if square:
            act(1, by_x)
            act(2, by_y)
        else:
            loop(1, chips, lambda m: act(m, lax.rem(j + 2 * m, bonds)))

    def early_copy(g, whole, m, i, to):
        at = piece(whole, i, m - 1)
        return remote(at, at, early_s.at[g, m - 1], early_r.at[g, m - 1], z, to)

    def rest_copy(g, whole, m, i, to):
        at = piece(whole, i, 2 - m)
        return remote(at, at, far_s.at[g, m], piece_r.at[g, i], z, to)

    def gather_start(g, whole):
        if square:
            each_far(lambda m, to: early_copy(g, whole, m, j, to).start())
            each_far(lambda m, to: rest_copy(g, whole, m, j, to).start())
        else:
            each_far(lambda m, to: far_copy(g, whole, m, to).start())
        near_copy(g, whole, j).start()

    def gather_pass(g, whole):
        def pass_on(m, i):
            early_copy(g, whole, m, i, twin).wait_recv()
            half_copy(g, whole, i, m - 1, by_y if m == 1 else by_x).start()

        def one(m, i):
            if square:
                rest_copy(g, whole, m, i, twin).wait_recv()
            else:
                arrived(g, whole, i)
            near_copy(g, whole, i).start()

        if square:
            each_far(pass_on)
        each_far(one)

    def gather_last(g, whole):
        if square:
            for half in range(2):
                half_copy(g, whole, by_xy, half, twin).wait_recv()
            near_copy(g, whole, by_xy).start()

    def gather_end(g, whole):
        loop(0, chips, lambda m: arrived(g, whole, lax.rem(twin + 2 * m, bonds)))

    def gather_sent(g, whole):
        if square:
            each_far(lambda m, to: early_copy(g, whole, m, j, to).wait_send())
            each_far(lambda m, to: rest_copy(g, whole, m, j, to).wait_send())
        else:
            each_far(lambda m, to: far_copy(g, whole, m, to).wait_send())
        if square:
            half_copy(g, whole, by_x, 0, by_y).wait_send()
            half_copy(g, whole, by_y, 1, by_x).wait_send()
        loop(0, chips, lambda m: near_copy(g, whole, lax.rem(j + 2 * m, bonds)).wait_send())

    gather_start(0, all_low)

    def swap(m):
        t = lax.rem(z + m, nodes)
        return remote(
            upper.at[t], own_up.at[:, pl.ds(pl.multiple_of(z * cols, cols), cols), :],
            swap_s.at[m], swap_r.at[z], t, j,
        )

    loop(1, nodes, lambda m: swap(m).start())

    def keep(p):
        own_up[p, pl.ds(pl.multiple_of(z * cols, cols), cols), :] = upper[z, p]

    loop(0, rows, keep)

    def grow(x_of, left_of, right_of):
        lefts = wide(jnp.concatenate([left_of(k).T for k in range(ops)], axis=0))

        def one(p, carry):
            out = halves(dot(lefts, twice(x_of(p))))
            for k in range(ops):
                grown[pl.ds(k * block + p, width, stride=rows), :] = out[k * width : (k + 1) * width]
            return carry

        lax.fori_loop(0, rows, one, 0, unroll=2)
        step = 4 * width
        for k in range(ops):
            right = twice(right_of(k))

            def chunk(i, carry):
                at = pl.ds(pl.multiple_of(k * block + i * step, step), step)
                grown[at, :] = halves(dot(wide(grown[at, :]), right))
                return carry

            lax.fori_loop(0, block // step, chunk, 0)

    def sides(g, x_of, left_of, right_of):
        rights = wide(jnp.concatenate([right_of(k).T for k in range(ops)], axis=0))

        def one(p, carry):
            turned = x_of(p).T
            out = halves(dot(rights, twice(turned)))
            turned_wide = wide(turned)
            at = pl.ds(pl.multiple_of(p * width, width), width)
            for k in range(ops):
                side_r[g, k, at, :] = wide(out[k * width : (k + 1) * width])
                high, low = split(halves(dot(turned_wide, twice(left_of(k)))))
                side_l[g, k, :width, at] = high
                side_l[g, k, width:, at] = low
            return carry

        lax.fori_loop(0, rows, one, 0, unroll=2)

    def column(whole, c):
        parts = [whole[pl.ds(pl.multiple_of(i * block + c * rows, rows), rows), :] for i in range(bonds)]
        return jnp.concatenate(parts, axis=0)

    def gram(g, whole):
        def slab(c):
            parts = [
                grown[pl.ds(pl.multiple_of(k * block + c * rows, rows), rows), :] for k in range(ops)
            ]
            return jnp.concatenate(split(jnp.concatenate(parts, axis=0)), axis=0)

        def one(i, acc):
            t = jnp.concatenate([slab(2 * i), slab(2 * i + 1)], axis=1)
            x = jnp.concatenate(
                [jnp.concatenate(split(column(whole, 2 * i + d)), axis=0) for d in range(2)], axis=1
            )
            return acc + dot(t, x, NT)

        zero = jnp.zeros((2 * packed, 2 * width), f32)
        out = lax.fori_loop(0, width // 2, one, zero, unroll=16)
        gram_s[g] = quarters(out).reshape(ops, rows, width)

    def band(i):
        return pl.ds(pl.multiple_of(i * rows, rows), rows)

    def sum_copy(k, m):
        i = lax.rem(j + m, bonds)
        return remote(
            part.at[0, k, :, band(i), :], got.at[k, j], sum_s.at[k, m], sum_r.at[k, j], z, i
        )

    def plane_sum(k):
        def add(m, acc):
            i = lax.rem(j + m, bonds)
            remote(
                part.at[0, k, :, mine, :], got.at[k, i], sum_s.at[k, 0], sum_r.at[k, i], z, twin
            ).wait_recv()
            return acc + got[k, i]

        return lax.fori_loop(1, bonds, add, part[0, k, :, mine, :])

    def env_target(first):
        number = jnp.where(z == 0, 1, 2 * z + first)
        low = (number >= nodes).astype(jnp.int32)
        return number - low * nodes, low, jnp.logical_or(z > 0, first == 0)

    def env_copy(k, first, i):
        plane, low, _ = env_target(first)
        return remote(
            part.at[1, k, first, band(i), :], parts_in.at[low, k, j],
            env_s.at[first, k, i], env_r.at[low, k, j], plane, i,
        )

    def env_each(k, act, keep_own):
        for first in range(2):
            plane, low, live = env_target(first)

            def one(i):
                own = plane * bonds + i == me

                @pl.when(jnp.logical_and(live, jnp.logical_not(own)))
                def _():
                    act(env_copy(k, first, i))

                if keep_own:
                    @pl.when(jnp.logical_and(live, own))
                    def _():
                        parts_in[low, k, j] = part[1, k, first, mine, :]

            loop(0, bonds, one)

    def env_send(k):
        env_each(k, lambda copy: copy.start(), True)

    def env_sent(k):
        env_each(k, lambda copy: copy.wait_send(), False)

    def env_wait(low):
        source = (nodes * low + z) // 2

        def operator(k):
            def add(i, acc):
                @pl.when(source * bonds + i != me)
                def _():
                    remote(
                        part.at[1, 0, 0, mine, :], parts_in.at[low, k, i],
                        env_s.at[0, 0, 0], env_r.at[low, k, i], z, twin,
                    ).wait_recv()

                return acc + parts_in[low, k, i]

            above[low, k] = lax.fori_loop(0, bonds, add, jnp.zeros((rows, width), f32))

        loop(0, ops, operator)

    def down(g, whole, env):
        e = jnp.concatenate(split(env.reshape(packed, width)), axis=0)
        e = jnp.concatenate([e, e], axis=1)

        def one(i, carry):
            x = jnp.concatenate(
                [jnp.concatenate(split(column(whole, 2 * i + d)), axis=0) for d in range(2)], axis=1
            )
            out = dot(e, x)
            out = out[:packed] + out[packed:]
            at = pl.multiple_of(2 * i * packed, packed)
            worked[pl.ds(at, packed), :] = out[:, :width]
            worked[pl.ds(at + packed, packed), :] = out[:, width:]
            return carry

        lax.fori_loop(0, width // 2, one, 0, unroll=16)

        def operator(k):
            def fill(p, carry):
                high, low = split(worked[pl.ds(k * rows + p, width, stride=packed), :])
                at = pl.ds(pl.multiple_of(p * width, width), width)
                long_l[:width, at] = high
                long_l[width:, at] = low
                long_r[at, :width] = high
                long_r[at, width:] = low
                return carry

            lax.fori_loop(0, rows, fill, 0, unroll=8)
            part[g, k, 0] = quarters(dot(long_l[...], side_r[g, k])).T
            part[g, k, 1] = quarters(dot(side_l[g, k], long_r[...]))
            if g == 0:
                loop(1, bonds, lambda m: sum_copy(k, m).start())
            else:
                env_send(k)

        loop(0, ops, operator)

    def child_copy(g, number, i):
        return remote(
            gram_s.at[g], childs.at[lax.rem(number, 2), :, mine, :],
            child_s.at[g, i], child_r.at[lax.rem(number, 2), j], number // 2, i,
        )

    def child_send(g, number):
        def one(i):
            own = (number // 2) * bonds + i == me

            @pl.when(own)
            def _():
                childs[lax.rem(number, 2), :, mine, :] = gram_s[g]

            @pl.when(jnp.logical_not(own))
            def _():
                child_copy(g, number, i).start()

        loop(0, bonds, one)

    def child_sent(g, number):
        def one(i):
            @pl.when((number // 2) * bonds + i != me)
            def _():
                child_copy(g, number, i).wait_send()

        loop(0, bonds, one)

    def child_wait():
        for first in range(2):
            number = 2 * z + first
            plane = jnp.where(number >= nodes, number - nodes, number)

            def one(i):
                @pl.when(plane * bonds + i != me)
                def _():
                    remote(
                        gram_s.at[0], childs.at[first, :, pl.ds(pl.multiple_of(i * rows, rows), rows), :],
                        child_s.at[0, 0], child_r.at[first, i], z, twin,
                    ).wait_recv()

            loop(0, bonds, one)

    grow(lambda p: bottom[0, p], lambda k: leaf[0, k, 0], lambda k: leaf[0, k, 1])
    gather_pass(0, all_low)

    def swapped(m):
        i = lax.rem(z + m, nodes)
        remote(
            upper.at[0], own_up.at[:, pl.ds(pl.multiple_of(i * cols, cols), cols), :],
            swap_s.at[0], swap_r.at[i], lax.rem(z + 1, nodes), j,
        ).wait_recv()

    loop(1, nodes, swapped)
    turn(own_up, all_up)
    gather_start(1, all_up)
    sides(0, lambda p: bottom[0, p], lambda k: leaf[0, k, 0], lambda k: leaf[0, k, 1])
    gather_last(0, all_low)
    gather_end(0, all_low)
    gram(0, all_low)
    child_send(0, nodes + z)

    def grow_up():
        grow(lambda p: own_up[p], lambda k: childs[0, k], lambda k: childs[1, k])

    def sides_up():
        sides(1, lambda p: own_up[p], lambda k: childs[0, k], lambda k: childs[1, k])

    gather_pass(1, all_up)

    @pl.when(z == 0)
    def _():
        childs[0] = outside[...]
        childs[1] = outside[...]
        above[0] = top[:, mine, :]
        sides_up()

    @pl.when(z > 1)
    def _():
        child_wait()
        grow_up()

    gather_last(1, all_up)
    gather_end(1, all_up)

    @pl.when(z > 1)
    def _():
        gram(1, all_up)
        child_send(1, z)

    @pl.when(z == 1)
    def _():
        child_wait()

    @pl.when(z > 0)
    def _():
        sides_up()
        env_wait(0)

    down(1, all_up, above[0])
    def root_copy(m):
        t = lax.rem(me + m, total)
        return remote(
            gram_s.at[1], root.at[:, mine, :], root_s.at[m], root_r.at[j], t // bonds, lax.rem(t, bonds)
        )

    @pl.when(z == 1)
    def _():
        grow_up()
        gram(1, all_up)
        root[:, mine, :] = gram_s[1]
        loop(1, total, lambda m: root_copy(m).start())

    env_wait(1)
    down(0, all_low, above[1])
    for k in range(ops):
        leaf_out[0, k] = plane_sum(k)

    def root_wait(i):
        @pl.when(bonds + i != me)
        def _():
            remote(
                gram_s.at[1], root.at[:, pl.ds(pl.multiple_of(i * rows, rows), rows), :],
                root_s.at[0], root_r.at[i], z, twin,
            ).wait_recv()

    loop(0, bonds, root_wait)
    root_out[...] = root[...]

    gather_sent(0, all_low)
    gather_sent(1, all_up)
    loop(1, nodes, lambda m: swap(m).wait_send())
    child_sent(0, nodes + z)

    @pl.when(z > 1)
    def _():
        child_sent(1, z)

    for k in range(ops):
        loop(1, bonds, lambda m: sum_copy(k, m).wait_send())
        env_sent(k)

    @pl.when(z == 1)
    def _():
        loop(1, total, lambda m: root_copy(m).wait_send())


def solution(mesh):
    nodes, bonds = mesh.shape["node"], mesh.shape["bond"]

    def local(bottom, upper, leaf, outside, top):
        rows, width = bottom.shape[1], bottom.shape[2]
        ops = leaf.shape[1]
        dma = pltpu.SemaphoreType.DMA
        return pl.pallas_call(
            functools.partial(kernel, nodes, bonds),
            out_shape=(
                jax.ShapeDtypeStruct((1, ops, 2, rows, width), f32),
                jax.ShapeDtypeStruct((ops, width, width), f32),
            ),
            in_specs=[pl.BlockSpec(memory_space=pltpu.VMEM)] * 5,
            out_specs=(pl.BlockSpec(memory_space=pltpu.VMEM),) * 2,
            scratch_shapes=[
                pltpu.VMEM((bonds * rows * width, width), f32),
                pltpu.VMEM((bonds * rows * width, width), f32),
                pltpu.VMEM((rows, width, width), f32),
                pltpu.VMEM((width * ops * rows, width), f32),
                pltpu.VMEM((width * ops * rows, width), f32),
                pltpu.VMEM((2, ops, rows * width, 2 * width), jnp.bfloat16),
                pltpu.VMEM((2, ops, 2 * width, rows * width), jnp.bfloat16),
                pltpu.VMEM((2 * width, rows * width), jnp.bfloat16),
                pltpu.VMEM((rows * width, 2 * width), jnp.bfloat16),
                pltpu.VMEM((2, ops, width, width), f32),
                pltpu.VMEM((2, ops, rows, width), f32),
                pltpu.VMEM((2, ops, 2, width, width), f32),
                pltpu.VMEM((ops, bonds, 2, rows, width), f32),
                pltpu.VMEM((2, ops, bonds, rows, width), f32),
                pltpu.VMEM((2, ops, rows, width), f32),
                pltpu.VMEM((ops, width, width), f32),
                dma((2, bonds // 2)),
                dma((2, bonds // 2)),
                dma((2, 2)),
                dma((2, 2)),
                dma((2, 2)),
                dma((2, 2)),
                dma((2, bonds)),
                dma((nodes,)),
                dma((nodes,)),
                dma((2, bonds)),
                dma((2, bonds)),
                dma((ops, bonds)),
                dma((ops, bonds)),
                dma((2, ops, bonds)),
                dma((2, ops, bonds)),
                dma((nodes * bonds,)),
                dma((bonds,)),
            ],
            compiler_params=pltpu.CompilerParams(
                collective_id=0, has_side_effects=True, vmem_limit_bytes=56 * 1024 * 1024
            ),
        )(bottom, upper, leaf, outside, top)

    placed = (
        P("node", "bond", None, None),
        P(None, "bond", "node", None),
        P("node", None, None, None, None),
        P(),
        P(),
    )
    return jax.shard_map(
        local,
        mesh=mesh,
        in_specs=placed,
        out_specs=(P("node", None, None, "bond", None), P()),
        check_vma=False,
    )
```

```python
import functools

import jax
import jax.numpy as jnp
from jax import lax
from jax.experimental import pallas as pl
from jax.experimental.pallas import tpu as pltpu
from jax.sharding import PartitionSpec as P

MESH = pl.DeviceIdType.MESH
NN = (((1,), (0,)), ((), ()))
NT = (((1,), (1,)), ((), ()))
f32 = jnp.float32


def split(x):
    high = x.astype(jnp.bfloat16)
    return high, (x - high.astype(f32)).astype(jnp.bfloat16)


def dot(a, b, dims=NN):
    return lax.dot_general(a, b, dims, preferred_element_type=f32)


def wide(x):
    return jnp.concatenate(split(x), axis=1)


def twice(x):
    w = wide(x)
    return jnp.concatenate([w, w], axis=0)


def halves(out):
    half = out.shape[1] // 2
    return out[:, :half] + out[:, half:]


def quarters(out):
    half = out.shape[0] // 2
    return halves(out[:half] + out[half:])


def loop(start, stop, body):
    def step(i, carry):
        body(i)
        return carry

    lax.fori_loop(start, stop, step, 0)


def kernel(
    nodes, bonds,
    bottom, upper, leaf, outside, top,
    leaf_out, root_out,
    all_low, all_up, own_up, grown, worked, side_r, side_l, long_l, long_r, childs, gram_s, part, got, parts_in, above, root,
    far_s, near_s, half_s, half_r, early_s, early_r, piece_r, swap_s, swap_r, child_s, child_r, sum_s, sum_r, env_s, env_r, root_s, root_r,
):
    z, j = lax.axis_index("node"), lax.axis_index("bond")
    me = z * bonds + j
    total = nodes * bonds
    chips = bonds // 2
    twin = j + 1 - 2 * lax.rem(j, 2)
    rows, width = bottom.shape[1], bottom.shape[2]
    ops = leaf.shape[1]
    cols = upper.shape[2]
    block = rows * width
    packed = ops * rows
    mine = pl.ds(pl.multiple_of(j * rows, rows), rows)

    def remote(src, dst, send, recv, plane, bond):
        return pltpu.make_async_remote_copy(
            src_ref=src, dst_ref=dst, send_sem=send, recv_sem=recv,
            device_id=(plane, bond), device_id_type=MESH,
        )

    barrier = pltpu.get_barrier_semaphore()

    def greet(m):
        t = lax.rem(me + m, total)
        pl.semaphore_signal(barrier, inc=1, device_id=(t // bonds, lax.rem(t, bonds)), device_id_type=MESH)

    loop(1, total, greet)

    def turn(src, dst):
        def one(p):
            dst[pl.ds(j * block + p, width, stride=rows), :] = src[p]

        loop(0, rows, one)

    turn(bottom.at[0], all_low)
    pl.semaphore_wait(barrier, total - 1)

    square = chips == 4
    by_x = j + 2 - 4 * lax.rem(j // 2, 2)
    turn_y = 4 - 8 * lax.rem(j // 4, 2)
    by_y, by_xy = j + turn_y, by_x + turn_y

    def piece(whole, i, half=None):
        if half is None:
            return whole.at[pl.ds(pl.multiple_of(i * block, block), block), :]
        size = block // 2
        return whole.at[pl.ds(pl.multiple_of(i * block + half * size, size), size), :]

    def far_copy(g, whole, m, to):
        return remote(piece(whole, j), piece(whole, j), far_s.at[g, m], piece_r.at[g, j], z, to)

    def near_copy(g, whole, i):
        return remote(piece(whole, i), piece(whole, i), near_s.at[g, i // 2], piece_r.at[g, i], z, twin)

    def half_copy(g, whole, i, half, to):
        return remote(
            piece(whole, i, half), piece(whole, i, half), half_s.at[g, half], half_r.at[g, half], z, to
        )

    def arrived(g, whole, i):
        remote(piece(whole, i), piece(whole, i), far_s.at[g, 0], piece_r.at[g, i], z, twin).wait_recv()

    def each_far(act):
        if square:
            act(1, by_x)
            act(2, by_y)
        else:
            loop(1, chips, lambda m: act(m, lax.rem(j + 2 * m, bonds)))

    def early_copy(g, whole, m, i, to):
        at = piece(whole, i, m - 1)
        return remote(at, at, early_s.at[g, m - 1], early_r.at[g, m - 1], z, to)

    def rest_copy(g, whole, m, i, to):
        at = piece(whole, i, 2 - m)
        return remote(at, at, far_s.at[g, m], piece_r.at[g, i], z, to)

    def gather_start(g, whole):
        if square:
            each_far(lambda m, to: early_copy(g, whole, m, j, to).start())
            each_far(lambda m, to: rest_copy(g, whole, m, j, to).start())
        else:
            each_far(lambda m, to: far_copy(g, whole, m, to).start())
        near_copy(g, whole, j).start()

    def gather_early(g, whole):
        def pass_on(m, i):
            early_copy(g, whole, m, i, twin).wait_recv()
            half_copy(g, whole, i, m - 1, by_y if m == 1 else by_x).start()

        if square:
            each_far(pass_on)

    def gather_pass(g, whole):
        def one(m, i):
            if square:
                rest_copy(g, whole, m, i, twin).wait_recv()
            else:
                arrived(g, whole, i)
            near_copy(g, whole, i).start()

        each_far(one)

    def gather_last(g, whole):
        if square:
            for half in range(2):
                half_copy(g, whole, by_xy, half, twin).wait_recv()
            near_copy(g, whole, by_xy).start()

    def gather_end(g, whole):
        loop(0, chips, lambda m: arrived(g, whole, lax.rem(twin + 2 * m, bonds)))

    def gather_sent(g, whole):
        if square:
            each_far(lambda m, to: early_copy(g, whole, m, j, to).wait_send())
            each_far(lambda m, to: rest_copy(g, whole, m, j, to).wait_send())
        else:
            each_far(lambda m, to: far_copy(g, whole, m, to).wait_send())
        if square:
            half_copy(g, whole, by_x, 0, by_y).wait_send()
            half_copy(g, whole, by_y, 1, by_x).wait_send()
        loop(0, chips, lambda m: near_copy(g, whole, lax.rem(j + 2 * m, bonds)).wait_send())

    gather_start(0, all_low)

    def swap(m):
        t = lax.rem(z + m, nodes)
        return remote(
            upper.at[t], own_up.at[:, pl.ds(pl.multiple_of(z * cols, cols), cols), :],
            swap_s.at[m], swap_r.at[z], t, j,
        )

    loop(1, nodes, lambda m: swap(m).start())

    def keep(p):
        own_up[p, pl.ds(pl.multiple_of(z * cols, cols), cols), :] = upper[z, p]

    loop(0, rows, keep)

    def grow(x_of, left_of, right_of):
        lefts = wide(jnp.concatenate([left_of(k).T for k in range(ops)], axis=0))

        def one(p, carry):
            out = halves(dot(lefts, twice(x_of(p))))
            for k in range(ops):
                grown[pl.ds(k * block + p, width, stride=rows), :] = out[k * width : (k + 1) * width]
            return carry

        lax.fori_loop(0, rows, one, 0, unroll=2)
        step = 4 * width
        for k in range(ops):
            right = twice(right_of(k))

            def chunk(i, carry):
                at = pl.ds(pl.multiple_of(k * block + i * step, step), step)
                grown[at, :] = halves(dot(wide(grown[at, :]), right))
                return carry

            lax.fori_loop(0, block // step, chunk, 0)

    def sides(g, x_of, left_of, right_of):
        rights = wide(jnp.concatenate([right_of(k).T for k in range(ops)], axis=0))

        def one(p, carry):
            turned = x_of(p).T
            out = halves(dot(rights, twice(turned)))
            turned_wide = wide(turned)
            at = pl.ds(pl.multiple_of(p * width, width), width)
            for k in range(ops):
                side_r[g, k, at, :] = wide(out[k * width : (k + 1) * width])
                high, low = split(halves(dot(turned_wide, twice(left_of(k)))))
                side_l[g, k, :width, at] = high
                side_l[g, k, width:, at] = low
            return carry

        lax.fori_loop(0, rows, one, 0, unroll=2)

    def column(whole, c):
        parts = [whole[pl.ds(pl.multiple_of(i * block + c * rows, rows), rows), :] for i in range(bonds)]
        return jnp.concatenate(parts, axis=0)

    def gram(g, whole):
        def slab(c):
            parts = [
                grown[pl.ds(pl.multiple_of(k * block + c * rows, rows), rows), :] for k in range(ops)
            ]
            return jnp.concatenate(split(jnp.concatenate(parts, axis=0)), axis=0)

        def one(i, acc):
            t = jnp.concatenate([slab(2 * i), slab(2 * i + 1)], axis=1)
            x = jnp.concatenate(
                [jnp.concatenate(split(column(whole, 2 * i + d)), axis=0) for d in range(2)], axis=1
            )
            return acc + dot(t, x, NT)

        zero = jnp.zeros((2 * packed, 2 * width), f32)
        out = lax.fori_loop(0, width // 2, one, zero, unroll=16)
        gram_s[g] = quarters(out).reshape(ops, rows, width)

    def band(i):
        return pl.ds(pl.multiple_of(i * rows, rows), rows)

    def sum_copy(k, m):
        i = lax.rem(j + m, bonds)
        return remote(
            part.at[0, k, :, band(i), :], got.at[k, j], sum_s.at[k, m], sum_r.at[k, j], z, i
        )

    def plane_sum(k):
        def add(m, acc):
            i = lax.rem(j + m, bonds)
            remote(
                part.at[0, k, :, mine, :], got.at[k, i], sum_s.at[k, 0], sum_r.at[k, i], z, twin
            ).wait_recv()
            return acc + got[k, i]

        return lax.fori_loop(1, bonds, add, part[0, k, :, mine, :])

    def env_target(first):
        number = jnp.where(z == 0, 1, 2 * z + first)
        low = (number >= nodes).astype(jnp.int32)
        return number - low * nodes, low, jnp.logical_or(z > 0, first == 0)

    def env_copy(k, first, i):
        plane, low, _ = env_target(first)
        return remote(
            part.at[1, k, first, band(i), :], parts_in.at[low, k, j],
            env_s.at[first, k, i], env_r.at[low, k, j], plane, i,
        )

    def env_each(k, act, keep_own):
        for first in range(2):
            plane, low, live = env_target(first)

            def one(i):
                own = plane * bonds + i == me

                @pl.when(jnp.logical_and(live, jnp.logical_not(own)))
                def _():
                    act(env_copy(k, first, i))

                if keep_own:
                    @pl.when(jnp.logical_and(live, own))
                    def _():
                        parts_in[low, k, j] = part[1, k, first, mine, :]

            loop(0, bonds, one)

    def env_send(k):
        env_each(k, lambda copy: copy.start(), True)

    def env_sent(k):
        env_each(k, lambda copy: copy.wait_send(), False)

    def env_wait(low):
        source = (nodes * low + z) // 2

        def operator(k):
            def add(i, acc):
                @pl.when(source * bonds + i != me)
                def _():
                    remote(
                        part.at[1, 0, 0, mine, :], parts_in.at[low, k, i],
                        env_s.at[0, 0, 0], env_r.at[low, k, i], z, twin,
                    ).wait_recv()

                return acc + parts_in[low, k, i]

            above[low, k] = lax.fori_loop(0, bonds, add, jnp.zeros((rows, width), f32))

        loop(0, ops, operator)

    def down(g, whole, env):
        e = jnp.concatenate(split(env.reshape(packed, width)), axis=0)
        e = jnp.concatenate([e, e], axis=1)

        def one(i, carry):
            x = jnp.concatenate(
                [jnp.concatenate(split(column(whole, 2 * i + d)), axis=0) for d in range(2)], axis=1
            )
            out = dot(e, x)
            out = out[:packed] + out[packed:]
            at = pl.multiple_of(2 * i * packed, packed)
            worked[pl.ds(at, packed), :] = out[:, :width]
            worked[pl.ds(at + packed, packed), :] = out[:, width:]
            return carry

        lax.fori_loop(0, width // 2, one, 0, unroll=16)

        def operator(k):
            def fill(p, carry):
                high, low = split(worked[pl.ds(k * rows + p, width, stride=packed), :])
                at = pl.ds(pl.multiple_of(p * width, width), width)
                long_l[:width, at] = high
                long_l[width:, at] = low
                long_r[at, :width] = high
                long_r[at, width:] = low
                return carry

            lax.fori_loop(0, rows, fill, 0, unroll=8)
            part[g, k, 0] = quarters(dot(long_l[...], side_r[g, k])).T
            part[g, k, 1] = quarters(dot(side_l[g, k], long_r[...]))
            if g == 0:
                loop(1, bonds, lambda m: sum_copy(k, m).start())
            else:
                env_send(k)

        loop(0, ops, operator)

    def child_copy(g, number, i):
        return remote(
            gram_s.at[g], childs.at[lax.rem(number, 2), :, mine, :],
            child_s.at[g, i], child_r.at[lax.rem(number, 2), j], number // 2, i,
        )

    def child_send(g, number):
        def one(i):
            own = (number // 2) * bonds + i == me

            @pl.when(own)
            def _():
                childs[lax.rem(number, 2), :, mine, :] = gram_s[g]

            @pl.when(jnp.logical_not(own))
            def _():
                child_copy(g, number, i).start()

        loop(0, bonds, one)

    def child_sent(g, number):
        def one(i):
            @pl.when((number // 2) * bonds + i != me)
            def _():
                child_copy(g, number, i).wait_send()

        loop(0, bonds, one)

    def child_wait():
        for first in range(2):
            number = 2 * z + first
            plane = jnp.where(number >= nodes, number - nodes, number)

            def one(i):
                @pl.when(plane * bonds + i != me)
                def _():
                    remote(
                        gram_s.at[0], childs.at[first, :, pl.ds(pl.multiple_of(i * rows, rows), rows), :],
                        child_s.at[0, 0], child_r.at[first, i], z, twin,
                    ).wait_recv()

            loop(0, bonds, one)

    grow(lambda p: bottom[0, p], lambda k: leaf[0, k, 0], lambda k: leaf[0, k, 1])
    gather_early(0, all_low)
    gather_pass(0, all_low)

    def swapped(m):
        i = lax.rem(z + m, nodes)
        remote(
            upper.at[0], own_up.at[:, pl.ds(pl.multiple_of(i * cols, cols), cols), :],
            swap_s.at[0], swap_r.at[i], lax.rem(z + 1, nodes), j,
        ).wait_recv()

    loop(1, nodes, swapped)
    turn(own_up, all_up)
    gather_start(1, all_up)
    sides(0, lambda p: bottom[0, p], lambda k: leaf[0, k, 0], lambda k: leaf[0, k, 1])
    gather_last(0, all_low)
    gather_end(0, all_low)
    gather_early(1, all_up)
    gram(0, all_low)
    child_send(0, nodes + z)

    def grow_up():
        grow(lambda p: own_up[p], lambda k: childs[0, k], lambda k: childs[1, k])

    def sides_up():
        sides(1, lambda p: own_up[p], lambda k: childs[0, k], lambda k: childs[1, k])

    gather_pass(1, all_up)

    @pl.when(z == 0)
    def _():
        childs[0] = outside[...]
        childs[1] = outside[...]
        above[0] = top[:, mine, :]
        sides_up()

    @pl.when(z > 1)
    def _():
        child_wait()
        grow_up()

    gather_last(1, all_up)
    gather_end(1, all_up)

    @pl.when(z > 1)
    def _():
        gram(1, all_up)
        child_send(1, z)

    @pl.when(z == 1)
    def _():
        child_wait()

    @pl.when(z > 0)
    def _():
        sides_up()
        env_wait(0)

    down(1, all_up, above[0])
    def root_copy(m):
        t = lax.rem(me + m, total)
        return remote(
            gram_s.at[1], root.at[:, mine, :], root_s.at[m], root_r.at[j], t // bonds, lax.rem(t, bonds)
        )

    @pl.when(z == 1)
    def _():
        grow_up()
        gram(1, all_up)
        root[:, mine, :] = gram_s[1]
        loop(1, total, lambda m: root_copy(m).start())

    env_wait(1)
    down(0, all_low, above[1])
    for k in range(ops):
        leaf_out[0, k] = plane_sum(k)

    def root_wait(i):
        @pl.when(bonds + i != me)
        def _():
            remote(
                gram_s.at[1], root.at[:, pl.ds(pl.multiple_of(i * rows, rows), rows), :],
                root_s.at[0], root_r.at[i], z, twin,
            ).wait_recv()

    loop(0, bonds, root_wait)
    root_out[...] = root[...]

    gather_sent(0, all_low)
    gather_sent(1, all_up)
    loop(1, nodes, lambda m: swap(m).wait_send())
    child_sent(0, nodes + z)

    @pl.when(z > 1)
    def _():
        child_sent(1, z)

    for k in range(ops):
        loop(1, bonds, lambda m: sum_copy(k, m).wait_send())
        env_sent(k)

    @pl.when(z == 1)
    def _():
        loop(1, total, lambda m: root_copy(m).wait_send())


def solution(mesh):
    nodes, bonds = mesh.shape["node"], mesh.shape["bond"]

    def local(bottom, upper, leaf, outside, top):
        rows, width = bottom.shape[1], bottom.shape[2]
        ops = leaf.shape[1]
        dma = pltpu.SemaphoreType.DMA
        return pl.pallas_call(
            functools.partial(kernel, nodes, bonds),
            out_shape=(
                jax.ShapeDtypeStruct((1, ops, 2, rows, width), f32),
                jax.ShapeDtypeStruct((ops, width, width), f32),
            ),
            in_specs=[pl.BlockSpec(memory_space=pltpu.VMEM)] * 5,
            out_specs=(pl.BlockSpec(memory_space=pltpu.VMEM),) * 2,
            scratch_shapes=[
                pltpu.VMEM((bonds * rows * width, width), f32),
                pltpu.VMEM((bonds * rows * width, width), f32),
                pltpu.VMEM((rows, width, width), f32),
                pltpu.VMEM((width * ops * rows, width), f32),
                pltpu.VMEM((width * ops * rows, width), f32),
                pltpu.VMEM((2, ops, rows * width, 2 * width), jnp.bfloat16),
                pltpu.VMEM((2, ops, 2 * width, rows * width), jnp.bfloat16),
                pltpu.VMEM((2 * width, rows * width), jnp.bfloat16),
                pltpu.VMEM((rows * width, 2 * width), jnp.bfloat16),
                pltpu.VMEM((2, ops, width, width), f32),
                pltpu.VMEM((2, ops, rows, width), f32),
                pltpu.VMEM((2, ops, 2, width, width), f32),
                pltpu.VMEM((ops, bonds, 2, rows, width), f32),
                pltpu.VMEM((2, ops, bonds, rows, width), f32),
                pltpu.VMEM((2, ops, rows, width), f32),
                pltpu.VMEM((ops, width, width), f32),
                dma((2, bonds // 2)),
                dma((2, bonds // 2)),
                dma((2, 2)),
                dma((2, 2)),
                dma((2, 2)),
                dma((2, 2)),
                dma((2, bonds)),
                dma((nodes,)),
                dma((nodes,)),
                dma((2, bonds)),
                dma((2, bonds)),
                dma((ops, bonds)),
                dma((ops, bonds)),
                dma((2, ops, bonds)),
                dma((2, ops, bonds)),
                dma((nodes * bonds,)),
                dma((bonds,)),
            ],
            compiler_params=pltpu.CompilerParams(
                collective_id=0, has_side_effects=True, vmem_limit_bytes=56 * 1024 * 1024
            ),
        )(bottom, upper, leaf, outside, top)

    placed = (
        P("node", "bond", None, None),
        P(None, "bond", "node", None),
        P("node", None, None, None, None),
        P(),
        P(),
    )
    return jax.shard_map(
        local,
        mesh=mesh,
        in_specs=placed,
        out_specs=(P("node", None, None, "bond", None), P()),
        check_vma=False,
    )
```
